32 devices in a mesh: dp: 4 (over y, core), fsdp: 4 (over z), seq: 2 (over x).
Axes of the slice: x: 2, y: 2, z: 4, core: 2. Of those that a mesh axis runs over, the one named last changes fastest.
Arguments:
- queries: bfloat16 [16, 256, 2048], P(('dp', 'fsdp'), 'seq'), may hold values from -30 to 30
- key_rows: bfloat16 [16, 256, 2048], P(('dp', 'fsdp'), 'seq'), may hold values from -12 to 12
- value_rows: bfloat16 [16, 256, 2048], P(('dp', 'fsdp'), 'seq'), may hold values from -6 to 6
- cotangent: bfloat16 [16, 256, 2048], P(('dp', 'fsdp'), 'seq'), may hold values from -6 to 6
- out_weight: bfloat16 [2048, 2048], P('fsdp'), may hold values from -0.125 to 0.125
Outputs:
- query_grad: bfloat16 [16, 256, 2048], P(('dp', 'fsdp'), 'seq')
- key_grad: bfloat16 [16, 256, 2048], P(('dp', 'fsdp'), 'seq')
- value_grad: bfloat16 [16, 256, 2048], P(('dp', 'fsdp'), 'seq')
- weight_grad: float32 [2048, 2048], P('fsdp')
The draws below stay inside these ranges and needn't reach their ends.
All inputs are finite; a program needn't handle non-finite values.
Results may differ from the reference program's by a relative error of at most 0.014.
Values may be sent and summed in bfloat16 or wider, within the bound.
A program may use at most 128 MiB of HBM per device.

```python
import jax
import jax.numpy as jnp
from jax import lax

D = 2048
H = 16
DH = 128
HD = 2048
SEQ_LEN = 256
SAMPLES = 16


def base_rows(key, salt):
    shape = (SAMPLES, SEQ_LEN, H * DH)
    entries = jnp.clip(jax.random.normal(jax.random.fold_in(key, salt), shape, jnp.float32), -4.0, 4.0)
    lows = jax.random.uniform(jax.random.fold_in(key, salt + 50), (SAMPLES, SEQ_LEN, 1), jnp.float32, jnp.log(0.3), jnp.log(3.0))
    return entries * jnp.exp(lows)


def draw_queries(key, part):
    base = base_rows(key, 21)
    return base.astype(jnp.bfloat16)


def draw_key_rows(key, part):
    base = base_rows(key, 22)
    return base.astype(jnp.bfloat16)


def steps_of(rng, extent, cuts, low, top_value):
    factor_of, own = 1.0, jax.random.fold_in(rng, 6)
    for position, parts in cuts:
        heights = jnp.exp(jax.random.uniform(jax.random.fold_in(own, position), (parts,), jnp.float32, low / len(cuts), top_value / len(cuts)))
        factor_of = factor_of * jnp.repeat(heights, extent[position] // parts).reshape([-1 if axis == position else 1 for axis in range(len(extent))])
    return factor_of


def centred(own_key, extent, spread, limit, split=(), kind=jnp.bfloat16):
    values = jax.random.normal(own_key, extent, jnp.float32) * spread
    if len(split) > 0:
        values = steps_of(own_key, extent, split, -0.22, 0.18) * values
    return jnp.clip(values, min=-limit, max=limit).astype(kind)


def setup_inputs(seed: int = 0) -> dict:
    key_of = jax.random.split(jax.random.key(seed), 6)
    return {
        "queries": draw_queries(jax.random.fold_in(key_of[5], 71), 0),
        "key_rows": draw_key_rows(jax.random.fold_in(key_of[5], 71), 0),
        "value_rows": centred(key_of[2], (SAMPLES, SEQ_LEN, HD), 1.0, 6.0, ((0, 16), (1, 2))),
        "cotangent": centred(key_of[3], (SAMPLES, SEQ_LEN, D), 1.0, 6.0, ((0, 16), (1, 2))),
        "out_weight": centred(key_of[4], (HD, D), HD ** -0.5, 0.125, ((0, 4),)),
    }


def head_backward(query_head, key_head, value_head, grad_head):
    score_scale = DH ** -0.5
    query_f = query_head.astype(jnp.float32)
    key_f = key_head.astype(jnp.float32)
    value_f = value_head.astype(jnp.float32)
    grad_f = grad_head.astype(jnp.float32)
    scores = jnp.dot(query_f, key_f.T) * score_scale
    highest = jnp.max(scores, axis=1, keepdims=True)
    expanded = jnp.exp(scores - highest)
    weights = expanded / jnp.sum(expanded, axis=1, keepdims=True)
    weights_half = weights.astype(jnp.bfloat16)
    weights_back = weights_half.astype(jnp.float32)
    attended = jnp.dot(weights_back, value_f).astype(jnp.bfloat16)
    grad_weights = jnp.dot(grad_f, value_f.T)
    row_delta = jnp.sum(weights * grad_weights, axis=1, keepdims=True)
    grad_scores = (weights * (grad_weights - row_delta)).astype(jnp.bfloat16).astype(jnp.float32)
    query_grad = (jnp.dot(grad_scores, key_f) * score_scale).astype(jnp.bfloat16)
    key_grad = (jnp.dot(grad_scores.T, query_f) * score_scale).astype(jnp.bfloat16)
    value_grad = jnp.dot(weights_back.T, grad_f).astype(jnp.bfloat16)
    return attended, query_grad, key_grad, value_grad


def split_heads(array):
    return array.reshape(SAMPLES, SEQ_LEN, H, DH).transpose(0, 2, 1, 3).reshape(SAMPLES * H, SEQ_LEN, DH)


def join_heads(array):
    return array.reshape(SAMPLES, H, SEQ_LEN, DH).transpose(0, 2, 1, 3).reshape(SAMPLES, SEQ_LEN, H * DH)


def reference(queries, key_rows, value_rows, cotangent, out_weight):
    flat_cot = cotangent.reshape(SAMPLES * SEQ_LEN, D).astype(jnp.float32)
    grad_out = jnp.dot(flat_cot, out_weight.astype(jnp.float32).T).astype(jnp.bfloat16)
    grad_out = grad_out.reshape(SAMPLES, SEQ_LEN, H * DH)
    stacked = (split_heads(queries), split_heads(key_rows), split_heads(value_rows), split_heads(grad_out))
    attended, query_grad, key_grad, value_grad = lax.map(lambda group: head_backward(*group), stacked)
    attended = join_heads(attended)
    flat_att = attended.reshape(SAMPLES * SEQ_LEN, H * DH).astype(jnp.float32)
    weight_grad = jnp.dot(flat_att.T, flat_cot) / SAMPLES
    return join_heads(query_grad), join_heads(key_grad), join_heads(value_grad), weight_grad
```

```python
import functools

import jax
import jax.numpy as jnp
from jax import lax
from jax.experimental import pallas as pl
from jax.experimental.pallas import tpu as pltpu
from jax.sharding import PartitionSpec as P

DH = 128
LOG2E = 1.4426950408889634
CHUNKS = 4
STORES = 8
F32 = jnp.float32
BF16 = jnp.bfloat16


def head_backward(query_head, key_head, value_head, grad_head, block_rows):
    length = key_head.shape[0]
    score_scale = DH ** (-0.5)
    blocks = length // block_rows

    def visit(carry, block):
        key_acc, value_acc = carry
        begin = block * block_rows
        query_block = lax.dynamic_slice_in_dim(query_head, begin, block_rows, 0)
        grad_block = lax.dynamic_slice_in_dim(grad_head, begin, block_rows, 0)
        scores = (
            jnp.einsum("qd,kd->qk", query_block, key_head, preferred_element_type=jnp.float32)
            * score_scale
        )
        highest = jnp.max(scores, axis=1, keepdims=True)
        expanded = jnp.exp(scores - highest)
        weights = expanded / jnp.sum(expanded, axis=1, keepdims=True)
        weights_half = weights.astype(jnp.bfloat16)
        attended = jnp.einsum(
            "qk,kd->qd", weights_half, value_head, preferred_element_type=jnp.float32
        ).astype(jnp.bfloat16)
        grad_weights = jnp.einsum(
            "qd,kd->qk", grad_block, value_head, preferred_element_type=jnp.float32
        )
        row_delta = jnp.sum(weights * grad_weights, axis=1, keepdims=True)
        grad_scores = (weights * (grad_weights - row_delta)).astype(jnp.bfloat16)
        query_grad = (
            jnp.einsum("qk,kd->qd", grad_scores, key_head, preferred_element_type=jnp.float32)
            * score_scale
        ).astype(jnp.bfloat16)
        key_acc = key_acc + jnp.einsum(
            "qk,qd->kd", grad_scores, query_block, preferred_element_type=jnp.float32
        )
        value_acc = value_acc + jnp.einsum(
            "qk,qd->kd", weights_half, grad_block, preferred_element_type=jnp.float32
        )
        return ((key_acc, value_acc), (attended, query_grad))

    empty = jnp.zeros(key_head.shape, jnp.float32)
    finals, stacked = lax.scan(visit, (empty, empty), jnp.arange(blocks))
    attended = stacked[0].reshape(length, DH)
    query_grad = stacked[1].reshape(length, DH)
    key_grad = (finals[0] * score_scale).astype(jnp.bfloat16)
    value_grad = finals[1].astype(jnp.bfloat16)
    return (attended, query_grad, key_grad, value_grad)


def attend_heads(query_heads, key_heads, value_heads, grad_heads):
    length = query_heads.shape[1]
    per_device = query_heads.shape[2] // DH
    block_rows = min(512, length)
    gathered = [[], [], [], []]
    for head_index in range(per_device):
        lower = head_index * DH
        upper = lower + DH
        results = head_backward(
            query_heads[0, :, lower:upper],
            key_heads[0, :, lower:upper],
            value_heads[0, :, lower:upper],
            grad_heads[0, :, lower:upper],
            block_rows,
        )
        for position, result in enumerate(results):
            gathered[position].append(result)
    return tuple((jnp.concatenate(group, axis=1)[None] for group in gathered))


def body(queries, key_rows, value_rows, cotangent, out_weight):
    samples = lax.axis_size("dp") * lax.axis_size("fsdp")
    grad_out = jnp.einsum(
        "btd,rd->btr",
        cotangent,
        lax.all_gather(out_weight, "fsdp", axis=0, tiled=True),
        preferred_element_type=jnp.float32,
    ).astype(jnp.bfloat16)
    query_heads, key_heads, value_heads, grad_heads = (
        lax.all_to_all(queries, "seq", split_axis=2, concat_axis=1, tiled=True),
        lax.all_to_all(key_rows, "seq", split_axis=2, concat_axis=1, tiled=True),
        lax.all_to_all(value_rows, "seq", split_axis=2, concat_axis=1, tiled=True),
        lax.all_to_all(grad_out, "seq", split_axis=2, concat_axis=1, tiled=True),
    )
    head_results = attend_heads(query_heads, key_heads, value_heads, grad_heads)
    attended, query_grad, key_grad, value_grad = (
        lax.all_to_all(head_results[0], "seq", split_axis=1, concat_axis=2, tiled=True),
        lax.all_to_all(head_results[1], "seq", split_axis=1, concat_axis=2, tiled=True),
        lax.all_to_all(head_results[2], "seq", split_axis=1, concat_axis=2, tiled=True),
        lax.all_to_all(head_results[3], "seq", split_axis=1, concat_axis=2, tiled=True),
    )
    shares = lax.psum_scatter(
        jnp.einsum("btr,btd->rd", attended, cotangent, preferred_element_type=jnp.float32),
        ("fsdp", "seq"),
        scatter_dimension=0,
        tiled=True,
    )
    shares = lax.psum(shares.astype(jnp.bfloat16), "dp").astype(jnp.float32)
    total = lax.all_gather(shares.astype(jnp.bfloat16), "seq", axis=0, tiled=True).astype(
        shares.dtype
    )
    return (query_grad, key_grad, value_grad, total / samples)


def dot_nn(a, b):
    return lax.dot_general(a, b, (((1,), (0,)), ((), ())), preferred_element_type=F32)


def dot_nt(a, b):
    return lax.dot_general(a, b, (((1,), (1,)), ((), ())), preferred_element_type=F32)


def dot_tn(a, b):
    return lax.dot_general(a, b, (((0,), (0,)), ((), ())), preferred_element_type=F32)


def fused_kernel(
    nf,
    q_hbm,
    k_hbm,
    v_hbm,
    c_hbm,
    w_hbm,
    gr_hbm,
    wg_hbm,
    cot,
    qkv,
    go_out,
    go_in,
    at_out,
    at_in,
    probs,
    grads,
    w_ref,
    acc,
    y_out,
    y_in,
    x_out,
    x_in,
    final,
    w_sem,
    in_send,
    in_recv,
    cot_z,
    cot_fw,
    cot_sib,
    cot_x,
    cot_recv,
    go_send,
    go_recv,
    at_send,
    at_recv,
    out_send,
    out_recv,
    rs_send,
    rs_recv,
    ag_send,
    ag_recv,
    wide_sem,
):
    tokens, width = c_hbm.shape
    rows = w_hbm.shape[0]
    part = width // CHUNKS
    core_rows = rows // 2
    half_rows = core_rows // 2
    group_heads = core_rows // DH
    length = 2 * tokens
    scale = DH ** (-0.5)
    dp = lax.axis_index("dp")
    f = lax.axis_index("fsdp")
    s = lax.axis_index("seq")
    core = dp % 2
    half = dp // 2
    twin = half * 2 + (1 - core)
    sibling = {"dp": twin}
    across = {"dp": (1 - half) * 2 + core}
    partner = {"seq": 1 - s}
    diagonal = {"dp": twin, "seq": 1 - s}
    native = core == s
    foreign = core != s
    inner = (f > 0) & (f < nf - 1)
    first = 1 + f % 2
    second = (2 + 3 * f) % 5
    third = 6 - f - first - second
    outer = 3 * (f - 1)

    def remote(src, dst, send, recv, device):
        return pltpu.make_async_remote_copy(
            src_ref=src,
            dst_ref=dst,
            send_sem=send,
            recv_sem=recv,
            device_id=device,
            device_id_type=pl.DeviceIdType.MESH,
        )

    def wait_into(ref, sem):
        pltpu.make_async_copy(ref, ref, sem).wait()

    def head_cols(g, c):
        return pl.ds(pl.multiple_of(g * rows + c * core_rows, core_rows), core_rows)

    def chunk(k):
        return c_hbm.at[:, k * part : (k + 1) * part]

    def group_at(i):
        return (f + 1 + i) % nf

    def near_local(which, g):
        src = (q_hbm, k_hbm, v_hbm)[which]
        return pltpu.make_async_copy(
            src.at[:, head_cols(g, core)], qkv.at[which, g, s], in_recv.at[which, g, s]
        )

    def near_copy(which, g):
        src = (q_hbm, k_hbm, v_hbm)[which]
        return remote(
            src.at[:, head_cols(g, core)],
            qkv.at[which, g, s],
            in_send.at[0, which, g],
            in_recv.at[which, g, s],
            {"seq": core},
        )

    def far_copy(which, g):
        src = (q_hbm, k_hbm, v_hbm)[which]
        return remote(
            src.at[:, head_cols(g, 1 - core)],
            qkv.at[which, g, s],
            in_send.at[1, which, g],
            in_recv.at[which, g, s],
            {"dp": twin, "seq": core},
        )

    def own_local(k):
        return pltpu.make_async_copy(chunk(k), cot.at[f, core, k], cot_recv.at[f, core, k])

    def own_z(lane, k, src):
        return remote(
            src,
            cot.at[f, core, k],
            cot_z.at[lane, k],
            cot_recv.at[f, core, k],
            {"fsdp": (first, second)[lane]},
        )

    def to_sibling(j, k, src):
        return remote(src, cot.at[j, core, k], cot_sib.at[j, k], cot_recv.at[j, core, k], sibling)

    def cross(k):
        return remote(
            chunk(k), cot.at[f, 1 - core, k], cot_x.at[k], cot_recv.at[f, 1 - core, k], diagonal
        )

    def passed(i):
        return (3 - f) + i * (3 - 2 * f)

    def pass_on(i, k):
        j = passed(i)
        block = cot.at[j, core, k]
        return remote(block, block, cot_fw.at[i, k], cot_recv.at[j, core, k], {"fsdp": outer})

    def go_copy(j):
        return remote(go_out.at[j], go_in.at[f], go_send.at[j], go_recv.at[f], {"fsdp": j})

    def at_copy(j):
        return remote(at_out.at[j], at_in.at[f], at_send.at[j], at_recv.at[f], {"fsdp": j})

    def home_local(g):
        return pltpu.make_async_copy(
            grads.at[g, s], gr_hbm.at[:, :, head_cols(g, core)], out_recv.at[g, core]
        )

    def home_copy(g, t):
        return remote(
            grads.at[g, t],
            gr_hbm.at[:, :, head_cols(g, core)],
            out_send.at[g, t],
            out_recv.at[g, core],
            {"dp": half * 2 + s, "seq": t},
        )

    w_load = pltpu.make_async_copy(
        w_hbm.at[pl.ds(pl.multiple_of(core * core_rows, core_rows), core_rows), :], w_ref, w_sem
    )

    @pl.when(native)
    def _():
        for i in range(nf):
            for which in range(3):
                near_local(which, group_at(i)).start()

    barrier = pltpu.get_barrier_semaphore()
    for device in (sibling, across, partner, diagonal):
        pl.semaphore_signal(
            barrier, inc=1, device_id=device, device_id_type=pl.DeviceIdType.MESH
        )
    for step in range(1, nf):
        pl.semaphore_signal(
            barrier,
            inc=1,
            device_id={"fsdp": (f + step) % nf},
            device_id_type=pl.DeviceIdType.MESH,
        )
    pl.semaphore_wait(barrier, 4 + nf - 1)

    @pl.when(native)
    def _():
        for which in range(3):
            far_copy(which, group_at(0)).start()
        for k in range(CHUNKS):
            own_z(0, k, chunk(k)).start()
            own_z(1, k, chunk(k)).start()
        for i in range(1, nf):
            for which in range(3):
                far_copy(which, group_at(i)).start()
        for k in range(CHUNKS):
            own_local(k).start()
            to_sibling(f, k, chunk(k)).start()

    @pl.when(foreign)
    def _():
        for i in range(nf):
            for which in range(3):
                near_copy(which, group_at(i)).start()
                far_copy(which, group_at(i)).start()
        for k in range(CHUNKS):
            cross(k).start()

    w_load.start()

    def head_of(which, g, inner_cols):
        return qkv[which, g, :, :, inner_cols].reshape(length, DH)

    def soften(i):
        g = group_at(i)
        for which in range(3):
            for t in range(2):
                wait_into(qkv.at[which, g, t], in_recv.at[which, g, t])
        for t in range(group_heads):
            cols = slice(t * DH, (t + 1) * DH)
            scores = dot_nt(head_of(0, g, cols), head_of(1, g, cols))
            highest = jnp.max(scores, axis=1, keepdims=True)
            expanded = jnp.exp2((scores - highest) * (scale * LOG2E))
            weights = expanded * (1.0 / jnp.sum(expanded, axis=1, keepdims=True))
            probs[g * group_heads + t] = weights
            at_out[g, :, cols] = dot_nn(weights.astype(BF16), head_of(2, g, cols)).astype(BF16)
        if i == nf - 1:
            at_in[f] = at_out[f]
        else:
            at_copy(g).start()

    def differentiate(g):
        for t in range(group_heads):
            cols = slice(t * DH, (t + 1) * DH)
            qh, kh, vh = (head_of(which, g, cols) for which in range(3))
            gh = go_in[g, :, cols]
            weights = probs[g * group_heads + t]
            grad_weights = dot_nt(gh, vh)
            delta = jnp.sum(weights * grad_weights, axis=1, keepdims=True)
            grad_scores = (weights * (grad_weights - delta)).astype(BF16)
            results = (
                dot_nn(grad_scores, kh) * scale,
                dot_tn(grad_scores, qh) * scale,
                dot_tn(weights.astype(BF16), gh),
            )
            for which, result in enumerate(results):
                grads[g, :, which, :, cols] = result.astype(BF16).reshape(2, tokens, DH)
        home_copy(g, 1 - s).start()

        @pl.when(native)
        def _():
            home_local(g).start()

        @pl.when(foreign)
        def _():
            home_copy(g, s).start()

    def project(j):
        total = None
        for k in range(CHUNKS):
            term = dot_nt(
                cot[j, :, k].reshape(length, part), w_ref[:, k * part : (k + 1) * part]
            )
            total = term if total is None else total + term
        return total.astype(BF16)

    def take(j, k):
        wait_into(cot.at[j, core, k], cot_recv.at[j, core, k])

    def take_other(j, k):
        wait_into(cot.at[j, 1 - core, k], cot_recv.at[j, 1 - core, k])

    def share(j, k):
        take(j, k)
        to_sibling(j, k, cot.at[j, core, k]).start()

    def urgent(k):
        @pl.when(inner)
        def _():
            for i in range(2):
                j = passed(i)
                take(j, k)
                pass_on(i, k).start()
                to_sibling(j, k, cot.at[j, core, k]).start()

    def relaxed(k):
        @pl.when(inner)
        def _():
            share(outer, k)

        @pl.when(jnp.logical_not(inner))
        def _():
            share(first, k)
            share(second, k)
            share(third, k)

    for i in range(nf):
        soften(i)

        @pl.when(native)
        def _():
            urgent(i)

    @pl.when(native)
    def _():
        for k in range(CHUNKS):
            take(f, k)
            relaxed(k)

    @pl.when(foreign)
    def _():
        for k in range(CHUNKS):
            take(f, k)
            own_z(0, k, cot.at[f, core, k]).start()
            own_z(1, k, cot.at[f, core, k]).start()
            to_sibling(f, k, cot.at[f, core, k]).start()

    for k in range(CHUNKS):
        take_other(f, k)
    w_load.wait()
    go_in[f] = project(f)
    differentiate(f)

    def mine():
        return pl.ds(pl.multiple_of(half * half_rows, half_rows), half_rows)

    def theirs():
        return pl.ds(pl.multiple_of((1 - half) * half_rows, half_rows), half_rows)

    def reduce_copy(stage, c):
        src, dst = ((y_out, y_in), (x_out, x_in))[stage]
        device = (across, partner)[stage]
        return remote(src.at[c], dst.at[c], rs_send.at[stage, c], rs_recv.at[stage, c], device)

    def gather_copy(stage, c):
        which = half if stage < 2 else 1 - half
        base = core * core_rows + which * half_rows
        block = final.at[c, pl.ds(pl.multiple_of(base, half_rows), half_rows)]
        device = (across, sibling, sibling)[stage]
        return remote(block, block, ag_send.at[stage, c], ag_recv.at[stage, c], device)

    def wide_copy(c):
        cols = slice(c * part, (c + 1) * part)
        return pltpu.make_async_copy(final.at[c], wg_hbm.at[:, cols], wide_sem.at[c])

    def weight_term(c):
        @pl.when(foreign)
        def _():
            urgent(c)
            relaxed(c)

        for d in (first, second, third):
            take_other(d, c)
        if c == 0:
            for d in (first, second, third):
                wait_into(at_in.at[d], at_recv.at[d])
        at_all = at_in[...].reshape(nf * length, core_rows)
        acc[c] = dot_tn(at_all, cot[:, :, c].reshape(nf * length, part))
        y_out[c] = acc[c, theirs()].astype(BF16)
        reduce_copy(0, c).start()

    def reduce_y(c):
        reduce_copy(0, c).wait_recv()
        x_out[c] = (acc[c, mine()] + y_in[c].astype(F32)).astype(BF16)
        reduce_copy(1, c).start()

    def reduce_x(c):
        reduce_copy(1, c).wait_recv()
        base = core * core_rows + half * half_rows
        final[c, pl.ds(pl.multiple_of(base, half_rows), half_rows)] = (
            x_out[c].astype(F32) + x_in[c].astype(F32)
        ).astype(BF16)
        gather_copy(0, c).start()
        gather_copy(1, c).start()

    def gather_y(c):
        gather_copy(0, c).wait_recv()
        gather_copy(2, c).start()

    def gather_core(c):
        gather_copy(1, c).wait_recv()
        gather_copy(2, c).wait_recv()
        wide_copy(c).start()

    def send_go(j):
        go_out[j] = project(j)
        go_copy(j).start()

    def take_go(j):
        wait_into(go_in.at[j], go_recv.at[j])
        differentiate(j)

    weight_term(0)
    weight_term(1)
    reduce_y(0)
    weight_term(2)
    reduce_y(1)
    reduce_x(0)
    weight_term(3)
    send_go(first)
    send_go(second)
    send_go(third)
    reduce_y(2)
    reduce_x(1)
    gather_y(0)
    reduce_y(3)
    take_go(first)
    reduce_x(2)
    gather_y(1)
    gather_core(0)
    reduce_x(3)
    take_go(second)
    gather_y(2)
    gather_core(1)
    gather_y(3)
    take_go(third)
    gather_core(2)
    gather_core(3)

    for g in range(nf):
        for c in range(2):
            wait_into(gr_hbm.at[:, :, head_cols(g, c)], out_recv.at[g, c])
    for c in range(CHUNKS):
        wide_copy(c).wait()

    for c in range(CHUNKS):
        for stage in range(2):
            reduce_copy(stage, c).wait_send()
        for stage in range(3):
            gather_copy(stage, c).wait_send()
    for j in (first, second, third):
        go_copy(j).wait_send()
        at_copy(j).wait_send()
    for g in range(nf):
        home_copy(g, 1 - s).wait_send()
        for which in range(3):
            far_copy(which, g).wait_send()
    for k in range(CHUNKS):
        own_z(0, k, cot.at[f, core, k]).wait_send()
        own_z(1, k, cot.at[f, core, k]).wait_send()
        for j in range(nf):
            to_sibling(j, k, cot.at[j, core, k]).wait_send()

    @pl.when(inner)
    def _():
        for k in range(CHUNKS):
            for i in range(2):
                pass_on(i, k).wait_send()

    @pl.when(foreign)
    def _():
        for g in range(nf):
            home_copy(g, s).wait_send()
            for which in range(3):
                near_copy(which, g).wait_send()
        for k in range(CHUNKS):
            cross(k).wait_send()


def store_kernel(
    factor,
    gr,
    wg,
    qg_out,
    kg_out,
    vg_out,
    wg_out,
    held,
    narrow,
    wide,
    sems,
    in_sems,
    out_sems,
):
    count = wg.shape[0] // STORES
    blocks = [slice(i * count, (i + 1) * count) for i in range(STORES)]
    loads = [
        pltpu.make_async_copy(wg.at[block], narrow.at[block], in_sems.at[i])
        for i, block in enumerate(blocks)
    ]
    fills = [pltpu.make_async_copy(gr.at[i], held.at[i], sems.at[0, i]) for i in range(3)]
    copies = [
        pltpu.make_async_copy(held.at[i], dst, sems.at[1, i])
        for i, dst in enumerate((qg_out, kg_out, vg_out))
    ]
    for copy in loads + fills:
        copy.start()
    for i, block in enumerate(blocks):
        loads[i].wait()
        wide[block, :] = narrow[block, :].astype(F32) * factor
        pltpu.make_async_copy(wide.at[block], wg_out.at[block], out_sems.at[i]).start()
    for fill, copy in zip(fills, copies):
        fill.wait()
        copy.start()
    for i, block in enumerate(blocks):
        pltpu.make_async_copy(wide.at[block], wg_out.at[block], out_sems.at[i]).wait()
    for copy in copies:
        copy.wait()


def fused_body(nf, queries, key_rows, value_rows, cotangent, out_weight):
    samples = lax.axis_size("dp") * nf
    tokens, heads_width = queries.shape[1:]
    rows, width = out_weight.shape
    part = width // CHUNKS
    core_rows = rows // 2
    half_rows = core_rows // 2
    length = 2 * tokens
    heads = heads_width // DH // 2
    dma = pltpu.SemaphoreType.DMA
    outs = pl.pallas_call(
        functools.partial(fused_kernel, nf),
        out_shape=(
            jax.ShapeDtypeStruct((3, tokens, heads_width), BF16),
            jax.ShapeDtypeStruct((rows, width), BF16),
        ),
        in_specs=[pl.BlockSpec(memory_space=pltpu.HBM)] * 5,
        out_specs=[pl.BlockSpec(memory_space=pltpu.HBM)] * 2,
        scratch_shapes=[
            pltpu.VMEM((nf, 2, CHUNKS, tokens, part), BF16),
            pltpu.VMEM((3, nf, 2, tokens, core_rows), BF16),
            pltpu.VMEM((nf, length, core_rows), BF16),
            pltpu.VMEM((nf, length, core_rows), BF16),
            pltpu.VMEM((nf, length, core_rows), BF16),
            pltpu.VMEM((nf, length, core_rows), BF16),
            pltpu.VMEM((heads, length, length), F32),
            pltpu.VMEM((nf, 2, 3, tokens, core_rows), BF16),
            pltpu.VMEM((core_rows, width), BF16),
            pltpu.VMEM((CHUNKS, core_rows, part), F32),
            pltpu.VMEM((CHUNKS, half_rows, part), BF16),
            pltpu.VMEM((CHUNKS, half_rows, part), BF16),
            pltpu.VMEM((CHUNKS, half_rows, part), BF16),
            pltpu.VMEM((CHUNKS, half_rows, part), BF16),
            pltpu.VMEM((CHUNKS, rows, part), BF16),
            dma,
            dma((2, 3, nf)),
            dma((3, nf, 2)),
            dma((2, CHUNKS)),
            dma((2, CHUNKS)),
            dma((nf, CHUNKS)),
            dma((CHUNKS,)),
            dma((nf, 2, CHUNKS)),
            dma((nf,)),
            dma((nf,)),
            dma((nf,)),
            dma((nf,)),
            dma((nf, 2)),
            dma((nf, 2)),
            dma((2, CHUNKS)),
            dma((2, CHUNKS)),
            dma((3, CHUNKS)),
            dma((3, CHUNKS)),
            dma((CHUNKS,)),
        ],
        compiler_params=pltpu.CompilerParams(
            collective_id=0, has_side_effects=True, vmem_limit_bytes=58 * 1024 * 1024
        ),
    )(queries[0], key_rows[0], value_rows[0], cotangent[0], out_weight)
    stored = pl.pallas_call(
        functools.partial(store_kernel, 1.0 / samples),
        out_shape=(jax.ShapeDtypeStruct((tokens, heads_width), BF16),) * 3
        + (jax.ShapeDtypeStruct((rows, width), F32),),
        in_specs=[pl.BlockSpec(memory_space=pltpu.HBM)] * 2,
        out_specs=[pl.BlockSpec(memory_space=pltpu.HBM)] * 4,
        scratch_shapes=[
            pltpu.VMEM((3, tokens, heads_width), BF16),
            pltpu.VMEM((rows, width), BF16),
            pltpu.VMEM((rows, width), F32),
            dma((2, 3)),
            dma((STORES,)),
            dma((STORES,)),
        ],
        compiler_params=pltpu.CompilerParams(vmem_limit_bytes=58 * 1024 * 1024),
    )(*outs)
    return tuple(out[None] for out in stored[:3]) + (stored[3],)


def pick_body(mesh):
    if mesh.shape["seq"] == 2 and mesh.shape["dp"] == 4 and mesh.shape["fsdp"] == 4:
        return functools.partial(fused_body, mesh.shape["fsdp"])
    return body


def solution(mesh):
    return jax.shard_map(
        pick_body(mesh),
        mesh=mesh,
        in_specs=(
            P(("dp", "fsdp"), "seq", None),
            P(("dp", "fsdp"), "seq", None),
            P(("dp", "fsdp"), "seq", None),
            P(("dp", "fsdp"), "seq", None),
            P("fsdp", None),
        ),
        out_specs=(
            P(("dp", "fsdp"), "seq", None),
            P(("dp", "fsdp"), "seq", None),
            P(("dp", "fsdp"), "seq", None),
            P("fsdp", None),
        ),
        check_vma=False,
    )
```

```python
import functools

import jax
import jax.numpy as jnp
from jax import lax
from jax.experimental import pallas as pl
from jax.experimental.pallas import tpu as pltpu
from jax.sharding import PartitionSpec as P

DH = 128
LOG2E = 1.4426950408889634
CHUNKS = 4
STORES = 8
F32 = jnp.float32
BF16 = jnp.bfloat16


def head_backward(query_head, key_head, value_head, grad_head, block_rows):
    length = key_head.shape[0]
    score_scale = DH ** (-0.5)
    blocks = length // block_rows

    def visit(carry, block):
        key_acc, value_acc = carry
        begin = block * block_rows
        query_block = lax.dynamic_slice_in_dim(query_head, begin, block_rows, 0)
        grad_block = lax.dynamic_slice_in_dim(grad_head, begin, block_rows, 0)
        scores = (
            jnp.einsum("qd,kd->qk", query_block, key_head, preferred_element_type=jnp.float32)
            * score_scale
        )
        highest = jnp.max(scores, axis=1, keepdims=True)
        expanded = jnp.exp(scores - highest)
        weights = expanded / jnp.sum(expanded, axis=1, keepdims=True)
        weights_half = weights.astype(jnp.bfloat16)
        attended = jnp.einsum(
            "qk,kd->qd", weights_half, value_head, preferred_element_type=jnp.float32
        ).astype(jnp.bfloat16)
        grad_weights = jnp.einsum(
            "qd,kd->qk", grad_block, value_head, preferred_element_type=jnp.float32
        )
        row_delta = jnp.sum(weights * grad_weights, axis=1, keepdims=True)
        grad_scores = (weights * (grad_weights - row_delta)).astype(jnp.bfloat16)
        query_grad = (
            jnp.einsum("qk,kd->qd", grad_scores, key_head, preferred_element_type=jnp.float32)
            * score_scale
        ).astype(jnp.bfloat16)
        key_acc = key_acc + jnp.einsum(
            "qk,qd->kd", grad_scores, query_block, preferred_element_type=jnp.float32
        )
        value_acc = value_acc + jnp.einsum(
            "qk,qd->kd", weights_half, grad_block, preferred_element_type=jnp.float32
        )
        return ((key_acc, value_acc), (attended, query_grad))

    empty = jnp.zeros(key_head.shape, jnp.float32)
    finals, stacked = lax.scan(visit, (empty, empty), jnp.arange(blocks))
    attended = stacked[0].reshape(length, DH)
    query_grad = stacked[1].reshape(length, DH)
    key_grad = (finals[0] * score_scale).astype(jnp.bfloat16)
    value_grad = finals[1].astype(jnp.bfloat16)
    return (attended, query_grad, key_grad, value_grad)


def attend_heads(query_heads, key_heads, value_heads, grad_heads):
    length = query_heads.shape[1]
    per_device = query_heads.shape[2] // DH
    block_rows = min(512, length)
    gathered = [[], [], [], []]
    for head_index in range(per_device):
        lower = head_index * DH
        upper = lower + DH
        results = head_backward(
            query_heads[0, :, lower:upper],
            key_heads[0, :, lower:upper],
            value_heads[0, :, lower:upper],
            grad_heads[0, :, lower:upper],
            block_rows,
        )
        for position, result in enumerate(results):
            gathered[position].append(result)
    return tuple((jnp.concatenate(group, axis=1)[None] for group in gathered))


def body(queries, key_rows, value_rows, cotangent, out_weight):
    samples = lax.axis_size("dp") * lax.axis_size("fsdp")
    grad_out = jnp.einsum(
        "btd,rd->btr",
        cotangent,
        lax.all_gather(out_weight, "fsdp", axis=0, tiled=True),
        preferred_element_type=jnp.float32,
    ).astype(jnp.bfloat16)
    query_heads, key_heads, value_heads, grad_heads = (
        lax.all_to_all(queries, "seq", split_axis=2, concat_axis=1, tiled=True),
        lax.all_to_all(key_rows, "seq", split_axis=2, concat_axis=1, tiled=True),
        lax.all_to_all(value_rows, "seq", split_axis=2, concat_axis=1, tiled=True),
        lax.all_to_all(grad_out, "seq", split_axis=2, concat_axis=1, tiled=True),
    )
    head_results = attend_heads(query_heads, key_heads, value_heads, grad_heads)
    attended, query_grad, key_grad, value_grad = (
        lax.all_to_all(head_results[0], "seq", split_axis=1, concat_axis=2, tiled=True),
        lax.all_to_all(head_results[1], "seq", split_axis=1, concat_axis=2, tiled=True),
        lax.all_to_all(head_results[2], "seq", split_axis=1, concat_axis=2, tiled=True),
        lax.all_to_all(head_results[3], "seq", split_axis=1, concat_axis=2, tiled=True),
    )
    shares = lax.psum_scatter(
        jnp.einsum("btr,btd->rd", attended, cotangent, preferred_element_type=jnp.float32),
        ("fsdp", "seq"),
        scatter_dimension=0,
        tiled=True,
    )
    shares = lax.psum(shares.astype(jnp.bfloat16), "dp").astype(jnp.float32)
    total = lax.all_gather(shares.astype(jnp.bfloat16), "seq", axis=0, tiled=True).astype(
        shares.dtype
    )
    return (query_grad, key_grad, value_grad, total / samples)


def dot_nn(a, b):
    return lax.dot_general(a, b, (((1,), (0,)), ((), ())), preferred_element_type=F32)


def dot_nt(a, b):
    return lax.dot_general(a, b, (((1,), (1,)), ((), ())), preferred_element_type=F32)


def dot_tn(a, b):
    return lax.dot_general(a, b, (((0,), (0,)), ((), ())), preferred_element_type=F32)


def fused_kernel(
    nf,
    q_hbm,
    k_hbm,
    v_hbm,
    c_hbm,
    w_hbm,
    gr_hbm,
    wg_hbm,
    cot,
    qkv,
    go_out,
    go_in,
    at_out,
    at_in,
    probs,
    grads,
    w_ref,
    acc,
    y_out,
    y_in,
    x_out,
    x_in,
    d_out,
    d_in,
    final,
    w_sem,
    in_send,
    in_recv,
    cot_z,
    cot_fw,
    cot_sib,
    cot_x,
    cot_recv,
    go_send,
    go_recv,
    at_send,
    at_recv,
    out_send,
    out_recv,
    rs_send,
    rs_recv,
    ag_send,
    ag_recv,
    ds_send,
    ds_recv,
    dg_send,
    dg_recv,
    df_send,
    df_recv,
    wide_sem,
):
    tokens, width = c_hbm.shape
    rows = w_hbm.shape[0]
    part = width // CHUNKS
    core_rows = rows // 2
    half_rows = core_rows // 2
    group_heads = core_rows // DH
    length = 2 * tokens
    scale = DH ** (-0.5)
    dp = lax.axis_index("dp")
    f = lax.axis_index("fsdp")
    s = lax.axis_index("seq")
    core = dp % 2
    half = dp // 2
    twin = half * 2 + (1 - core)
    sibling = {"dp": twin}
    across = {"dp": (1 - half) * 2 + core}
    partner = {"seq": 1 - s}
    diagonal = {"dp": twin, "seq": 1 - s}
    native = core == s
    foreign = core != s
    inner = (f > 0) & (f < nf - 1)
    first = 1 + f % 2
    second = (2 + 3 * f) % 5
    third = 6 - f - first - second
    end = 3 * (f - 1)
    outer = jnp.logical_not(inner)
    corner = {"dp": (1 - half) * 2 + core, "seq": 1 - s}

    def remote(src, dst, send, recv, device):
        return pltpu.make_async_remote_copy(
            src_ref=src,
            dst_ref=dst,
            send_sem=send,
            recv_sem=recv,
            device_id=device,
            device_id_type=pl.DeviceIdType.MESH,
        )

    def wait_into(ref, sem):
        pltpu.make_async_copy(ref, ref, sem).wait()

    def head_cols(g, c):
        return pl.ds(pl.multiple_of(g * rows + c * core_rows, core_rows), core_rows)

    def chunk(k):
        return c_hbm.at[:, k * part : (k + 1) * part]

    def group_at(i):
        return (f + 1 + i) % nf

    def near_local(which, g):
        src = (q_hbm, k_hbm, v_hbm)[which]
        return pltpu.make_async_copy(
            src.at[:, head_cols(g, core)], qkv.at[which, g, s], in_recv.at[which, g, s]
        )

    def near_copy(which, g):
        src = (q_hbm, k_hbm, v_hbm)[which]
        return remote(
            src.at[:, head_cols(g, core)],
            qkv.at[which, g, s],
            in_send.at[0, which, g],
            in_recv.at[which, g, s],
            {"seq": core},
        )

    def far_copy(which, g):
        src = (q_hbm, k_hbm, v_hbm)[which]
        return remote(
            src.at[:, head_cols(g, 1 - core)],
            qkv.at[which, g, s],
            in_send.at[1, which, g],
            in_recv.at[which, g, s],
            {"dp": twin, "seq": core},
        )

    def own_local(k):
        return pltpu.make_async_copy(chunk(k), cot.at[f, core, k], cot_recv.at[f, core, k])

    def own_z(lane, k, src):
        return remote(
            src,
            cot.at[f, core, k],
            cot_z.at[lane, k],
            cot_recv.at[f, core, k],
            {"fsdp": (first, second)[lane]},
        )

    def to_sibling(j, k, src):
        return remote(src, cot.at[j, core, k], cot_sib.at[j, k], cot_recv.at[j, core, k], sibling)

    def cross(k):
        return remote(
            chunk(k), cot.at[f, 1 - core, k], cot_x.at[k], cot_recv.at[f, 1 - core, k], diagonal
        )

    def passed(i):
        return (3 - f) + i * (3 - 2 * f)

    def pass_on(i, k):
        j = passed(i)
        block = cot.at[j, core, k]
        return remote(block, block, cot_fw.at[i, k], cot_recv.at[j, core, k], {"fsdp": end})

    def go_copy(j):
        return remote(go_out.at[j], go_in.at[f], go_send.at[j], go_recv.at[f], {"fsdp": j})

    def at_copy(j):
        return remote(at_out.at[j], at_in.at[f], at_send.at[j], at_recv.at[f], {"fsdp": j})

    def home_local(g):
        return pltpu.make_async_copy(
            grads.at[g, s], gr_hbm.at[:, :, head_cols(g, core)], out_recv.at[g, core]
        )

    def home_copy(g, t):
        return remote(
            grads.at[g, t],
            gr_hbm.at[:, :, head_cols(g, core)],
            out_send.at[g, t],
            out_recv.at[g, core],
            {"dp": half * 2 + s, "seq": t},
        )

    w_load = pltpu.make_async_copy(
        w_hbm.at[pl.ds(pl.multiple_of(core * core_rows, core_rows), core_rows), :], w_ref, w_sem
    )

    @pl.when(native)
    def _():
        for i in range(nf):
            for which in range(3):
                near_local(which, group_at(i)).start()

    barrier = pltpu.get_barrier_semaphore()
    for device in (sibling, across, partner, diagonal, corner):
        pl.semaphore_signal(
            barrier, inc=1, device_id=device, device_id_type=pl.DeviceIdType.MESH
        )
    for step in range(1, nf):
        pl.semaphore_signal(
            barrier,
            inc=1,
            device_id={"fsdp": (f + step) % nf},
            device_id_type=pl.DeviceIdType.MESH,
        )
    pl.semaphore_wait(barrier, 5 + nf - 1)

    @pl.when(native)
    def _():
        for k in range(CHUNKS):
            own_z(0, k, chunk(k)).start()
            own_z(1, k, chunk(k)).start()
        for i in range(nf):
            for which in range(3):
                far_copy(which, group_at(i)).start()
        for k in range(CHUNKS):
            own_local(k).start()
            to_sibling(f, k, chunk(k)).start()

    @pl.when(foreign)
    def _():
        for i in range(nf):
            for which in range(3):
                near_copy(which, group_at(i)).start()
                far_copy(which, group_at(i)).start()
            cross(i).start()

    w_load.start()

    def head_of(which, g, inner_cols):
        return qkv[which, g, :, :, inner_cols].reshape(length, DH)

    def soften(i):
        g = group_at(i)
        for which in range(3):
            for t in range(2):
                wait_into(qkv.at[which, g, t], in_recv.at[which, g, t])
        for t in range(group_heads):
            cols = slice(t * DH, (t + 1) * DH)
            scores = dot_nt(head_of(0, g, cols), head_of(1, g, cols))
            highest = jnp.max(scores, axis=1, keepdims=True)
            expanded = jnp.exp2((scores - highest) * (scale * LOG2E))
            weights = expanded * (1.0 / jnp.sum(expanded, axis=1, keepdims=True))
            probs[g * group_heads + t] = weights
            at_out[g, :, cols] = dot_nn(weights.astype(BF16), head_of(2, g, cols)).astype(BF16)
        if i == nf - 1:
            at_in[f] = at_out[f]
        else:
            at_copy(g).start()

    def differentiate(g):
        for t in range(group_heads):
            cols = slice(t * DH, (t + 1) * DH)
            qh, kh, vh = (head_of(which, g, cols) for which in range(3))
            gh = go_in[g, :, cols]
            weights = probs[g * group_heads + t]
            grad_weights = dot_nt(gh, vh)
            delta = jnp.sum(weights * grad_weights, axis=1, keepdims=True)
            grad_scores = (weights * (grad_weights - delta)).astype(BF16)
            results = (
                dot_nn(grad_scores, kh) * scale,
                dot_tn(grad_scores, qh) * scale,
                dot_tn(weights.astype(BF16), gh),
            )
            for which, result in enumerate(results):
                grads[g, :, which, :, cols] = result.astype(BF16).reshape(2, tokens, DH)
        home_copy(g, 1 - s).start()

        @pl.when(native)
        def _():
            home_local(g).start()

        @pl.when(foreign)
        def _():
            home_copy(g, s).start()

    def project(j):
        total = None
        for k in range(CHUNKS):
            term = dot_nt(
                cot[j, :, k].reshape(length, part), w_ref[:, k * part : (k + 1) * part]
            )
            total = term if total is None else total + term
        return total.astype(BF16)

    def take(j, k):
        wait_into(cot.at[j, core, k], cot_recv.at[j, core, k])

    def take_other(j, k):
        wait_into(cot.at[j, 1 - core, k], cot_recv.at[j, 1 - core, k])

    def share(j, k):
        take(j, k)
        to_sibling(j, k, cot.at[j, core, k]).start()

    def urgent(k):
        @pl.when(inner)
        def _():
            for i in range(2):
                j = passed(i)
                take(j, k)
                pass_on(i, k).start()
                to_sibling(j, k, cot.at[j, core, k]).start()

    def pass_own(k):
        take(f, k)
        own_z(0, k, cot.at[f, core, k]).start()
        own_z(1, k, cot.at[f, core, k]).start()
        to_sibling(f, k, cot.at[f, core, k]).start()

    def for_native(*chunks):
        @pl.when(native)
        def _():
            for k in chunks:
                urgent(k)

    def for_foreign(*chunks):
        @pl.when(foreign)
        def _():
            for k in chunks:
                urgent(k)

    def for_own(k):
        @pl.when(foreign)
        def _():
            pass_own(k)

    for_native(0)
    soften(0)
    for_native(1)
    for_own(0)
    soften(1)
    for_native(2)
    for_own(1)
    soften(2)
    for_native(3)
    for_own(2)
    for_foreign(0)
    soften(3)
    for_own(3)

    @pl.when(native)
    def _():
        for k in range(CHUNKS):
            take(f, k)

    for k in range(CHUNKS):
        take_other(f, k)
    w_load.wait()
    go_in[f] = project(f)
    differentiate(f)

    def mine():
        return pl.ds(pl.multiple_of(half * half_rows, half_rows), half_rows)

    def theirs():
        return pl.ds(pl.multiple_of((1 - half) * half_rows, half_rows), half_rows)

    def reduce_copy(stage, c):
        src, dst = ((y_out, y_in), (x_out, x_in))[stage]
        device = (across, partner)[stage]
        return remote(src.at[c], dst.at[c], rs_send.at[stage, c], rs_recv.at[stage, c], device)

    def gather_copy(stage, c):
        which = half if stage < 2 else 1 - half
        base = core * core_rows + which * half_rows
        block = final.at[c, pl.ds(pl.multiple_of(base, half_rows), half_rows)]
        device = (across, sibling, sibling)[stage]
        return remote(block, block, ag_send.at[stage, c], ag_recv.at[stage, c], device)

    def wide_copy(c):
        cols = slice(c * part, (c + 1) * part)
        return pltpu.make_async_copy(final.at[c], wg_hbm.at[:, cols], wide_sem.at[c])

    last = CHUNKS - 1

    def quarter_of(h, t):
        count = half_rows // 2
        return pl.ds(pl.multiple_of((h * 2 + t) * count, count), count)

    others = ((half, 1 - s, partner), (1 - half, s, across), (1 - half, 1 - s, corner))

    def direct_copy(i):
        h, t, device = others[i]
        return remote(d_out.at[quarter_of(h, t)], d_in.at[i], ds_send.at[i], ds_recv.at[i], device)

    def piece(c, h, t):
        base = core * core_rows + (h * 2 + t) * (half_rows // 2)
        return final.at[last, pl.ds(pl.multiple_of(base, half_rows // 2), half_rows // 2)]

    def spread_copy(i):
        block = piece(core, half, s)
        device = (partner, across, corner, sibling)[i]
        return remote(block, block, dg_send.at[i], dg_recv.at[i], device)

    def relay_copy(i):
        h, t, _ = others[i]
        block = piece(core, h, t)
        return remote(block, block, df_send.at[i], df_recv.at[i], sibling)

    def weight_term(c):
        if c == 0:
            for d in (first, second, third):
                wait_into(at_in.at[d], at_recv.at[d])
        at_all = at_in[...].reshape(nf * length, core_rows)
        acc[c] = dot_tn(at_all, cot[:, :, c].reshape(nf * length, part))
        if c < last:
            y_out[c] = acc[c, theirs()].astype(BF16)
            reduce_copy(0, c).start()
        else:
            d_out[...] = acc[c].astype(BF16)
            for i in (2, 1, 0):
                direct_copy(i).start()

    def reduce_direct(c):
        total = acc[last, quarter_of(half, s)]
        for i in range(3):
            direct_copy(i).wait_recv()
            total = total + d_in[i].astype(F32)
        piece(core, half, s)[...] = total.astype(BF16)
        for i in (2, 1, 0, 3):
            spread_copy(i).start()

    def gather_direct(c):
        for i in range(3):
            spread_copy(i).wait_recv()
            relay_copy(i).start()

    def gather_last(c):
        spread_copy(3).wait_recv()
        for i in range(3):
            relay_copy(i).wait_recv()
        wide_copy(last).start()

    def reduce_y(c):
        reduce_copy(0, c).wait_recv()
        x_out[c] = (acc[c, mine()] + y_in[c].astype(F32)).astype(BF16)
        reduce_copy(1, c).start()

    def reduce_x(c):
        reduce_copy(1, c).wait_recv()
        base = core * core_rows + half * half_rows
        final[c, pl.ds(pl.multiple_of(base, half_rows), half_rows)] = (
            x_out[c].astype(F32) + x_in[c].astype(F32)
        ).astype(BF16)
        gather_copy(0, c).start()
        gather_copy(1, c).start()

    def gather_y(c):
        gather_copy(0, c).wait_recv()
        gather_copy(2, c).start()

    def gather_core(c):
        gather_copy(1, c).wait_recv()
        gather_copy(2, c).wait_recv()
        wide_copy(c).start()

    def send_go(j):
        go_out[j] = project(j)
        go_copy(j).start()

    def take_go(j):
        wait_into(go_in.at[j], go_recv.at[j])
        differentiate(j)

    def arrive(j, k):
        share(j, k)
        take_other(j, k)

    def all_arrive(k):
        for j in (first, second, third):
            share(j, k)
        for j in (first, second, third):
            take_other(j, k)

    def end_arrives(k):
        arrive(second, k)

    def passed_arrive(k):
        if k > 0:
            for_foreign(k)
        take_other(first, k)
        take_other(third, k)

    def play(*steps):
        for action, argument in steps:
            action(argument)

    @pl.when(inner)
    def _():
        play(
            (end_arrives, 0),
            (passed_arrive, 0),
            (weight_term, 0),
            (end_arrives, 1),
            (passed_arrive, 1),
            (weight_term, 1),
            (end_arrives, 2),
            (end_arrives, 3),
            (send_go, second),
            (reduce_y, 0),
            (passed_arrive, 2),
            (weight_term, 2),
            (reduce_y, 1),
            (passed_arrive, 3),
            (weight_term, 3),
            (send_go, third),
            (send_go, first),
            (reduce_x, 0),
            (reduce_y, 2),
            (take_go, first),
            (reduce_x, 1),
            (gather_y, 0),
            (reduce_direct, last),
            (reduce_x, 2),
            (gather_y, 1),
            (gather_core, 0),
            (take_go, third),
            (gather_direct, last),
            (take_go, second),
            (gather_y, 2),
            (gather_core, 1),
            (gather_last, last),
            (gather_core, 2),
        )

    @pl.when(outer)
    def _():
        play(
            (all_arrive, 0),
            (weight_term, 0),
            (all_arrive, 1),
            (weight_term, 1),
            (reduce_y, 0),
            (take_go, first),
            (all_arrive, 2),
            (weight_term, 2),
            (reduce_y, 1),
            (reduce_x, 0),
            (all_arrive, 3),
            (weight_term, 3),
            (send_go, third),
            (send_go, second),
            (send_go, first),
            (reduce_y, 2),
            (reduce_x, 1),
            (gather_y, 0),
            (take_go, second),
            (reduce_direct, last),
            (gather_y, 1),
            (gather_core, 0),
            (take_go, third),
            (reduce_x, 2),
            (gather_direct, last),
            (gather_core, 1),
            (gather_y, 2),
            (gather_last, last),
            (gather_core, 2),
        )

    for g in range(nf):
        for c in range(2):
            wait_into(gr_hbm.at[:, :, head_cols(g, c)], out_recv.at[g, c])
    for c in range(CHUNKS):
        wide_copy(c).wait()

    for c in range(CHUNKS):
        if c == last:
            continue
        for stage in range(2):
            reduce_copy(stage, c).wait_send()
        for stage in range(3):
            gather_copy(stage, c).wait_send()
    for i in range(3):
        direct_copy(i).wait_send()
        relay_copy(i).wait_send()
    for i in range(4):
        spread_copy(i).wait_send()
    for j in (first, second, third):
        go_copy(j).wait_send()
        at_copy(j).wait_send()
    for g in range(nf):
        home_copy(g, 1 - s).wait_send()
        for which in range(3):
            far_copy(which, g).wait_send()
    for k in range(CHUNKS):
        own_z(0, k, cot.at[f, core, k]).wait_send()
        own_z(1, k, cot.at[f, core, k]).wait_send()
        for j in range(nf):
            to_sibling(j, k, cot.at[j, core, k]).wait_send()

    @pl.when(inner)
    def _():
        for k in range(CHUNKS):
            for i in range(2):
                pass_on(i, k).wait_send()

    @pl.when(foreign)
    def _():
        for g in range(nf):
            home_copy(g, s).wait_send()
            for which in range(3):
                near_copy(which, g).wait_send()
        for k in range(CHUNKS):
            cross(k).wait_send()


def store_kernel(
    factor,
    gr,
    wg,
    qg_out,
    kg_out,
    vg_out,
    wg_out,
    held,
    narrow,
    wide,
    sems,
    in_sems,
    out_sems,
):
    count = wg.shape[0] // STORES
    blocks = [slice(i * count, (i + 1) * count) for i in range(STORES)]
    loads = [
        pltpu.make_async_copy(wg.at[block], narrow.at[block], in_sems.at[i])
        for i, block in enumerate(blocks)
    ]
    fills = [pltpu.make_async_copy(gr.at[i], held.at[i], sems.at[0, i]) for i in range(3)]
    copies = [
        pltpu.make_async_copy(held.at[i], dst, sems.at[1, i])
        for i, dst in enumerate((qg_out, kg_out, vg_out))
    ]
    for copy in loads + fills:
        copy.start()
    for i, block in enumerate(blocks):
        loads[i].wait()
        wide[block, :] = narrow[block, :].astype(F32) * factor
        pltpu.make_async_copy(wide.at[block], wg_out.at[block], out_sems.at[i]).start()
    for fill, copy in zip(fills, copies):
        fill.wait()
        copy.start()
    for i, block in enumerate(blocks):
        pltpu.make_async_copy(wide.at[block], wg_out.at[block], out_sems.at[i]).wait()
    for copy in copies:
        copy.wait()


def fused_body(nf, queries, key_rows, value_rows, cotangent, out_weight):
    samples = lax.axis_size("dp") * nf
    tokens, heads_width = queries.shape[1:]
    rows, width = out_weight.shape
    part = width // CHUNKS
    core_rows = rows // 2
    half_rows = core_rows // 2
    length = 2 * tokens
    heads = heads_width // DH // 2
    dma = pltpu.SemaphoreType.DMA
    outs = pl.pallas_call(
        functools.partial(fused_kernel, nf),
        out_shape=(
            jax.ShapeDtypeStruct((3, tokens, heads_width), BF16),
            jax.ShapeDtypeStruct((rows, width), BF16),
        ),
        in_specs=[pl.BlockSpec(memory_space=pltpu.HBM)] * 5,
        out_specs=[pl.BlockSpec(memory_space=pltpu.HBM)] * 2,
        scratch_shapes=[
            pltpu.VMEM((nf, 2, CHUNKS, tokens, part), BF16),
            pltpu.VMEM((3, nf, 2, tokens, core_rows), BF16),
            pltpu.VMEM((nf, length, core_rows), BF16),
            pltpu.VMEM((nf, length, core_rows), BF16),
            pltpu.VMEM((nf, length, core_rows), BF16),
            pltpu.VMEM((nf, length, core_rows), BF16),
            pltpu.VMEM((heads, length, length), F32),
            pltpu.VMEM((nf, 2, 3, tokens, core_rows), BF16),
            pltpu.VMEM((core_rows, width), BF16),
            pltpu.VMEM((CHUNKS, core_rows, part), F32),
            pltpu.VMEM((CHUNKS, half_rows, part), BF16),
            pltpu.VMEM((CHUNKS, half_rows, part), BF16),
            pltpu.VMEM((CHUNKS, half_rows, part), BF16),
            pltpu.VMEM((CHUNKS, half_rows, part), BF16),
            pltpu.VMEM((core_rows, part), BF16),
            pltpu.VMEM((3, half_rows // 2, part), BF16),
            pltpu.VMEM((CHUNKS, rows, part), BF16),
            dma,
            dma((2, 3, nf)),
            dma((3, nf, 2)),
            dma((2, CHUNKS)),
            dma((2, CHUNKS)),
            dma((nf, CHUNKS)),
            dma((CHUNKS,)),
            dma((nf, 2, CHUNKS)),
            dma((nf,)),
            dma((nf,)),
            dma((nf,)),
            dma((nf,)),
            dma((nf, 2)),
            dma((nf, 2)),
            dma((2, CHUNKS)),
            dma((2, CHUNKS)),
            dma((3, CHUNKS)),
            dma((3, CHUNKS)),
            dma((3,)),
            dma((3,)),
            dma((4,)),
            dma((4,)),
            dma((3,)),
            dma((3,)),
            dma((CHUNKS,)),
        ],
        compiler_params=pltpu.CompilerParams(
            collective_id=0, has_side_effects=True, vmem_limit_bytes=58 * 1024 * 1024
        ),
    )(queries[0], key_rows[0], value_rows[0], cotangent[0], out_weight)
    stored = pl.pallas_call(
        functools.partial(store_kernel, 1.0 / samples),
        out_shape=(jax.ShapeDtypeStruct((tokens, heads_width), BF16),) * 3
        + (jax.ShapeDtypeStruct((rows, width), F32),),
        in_specs=[pl.BlockSpec(memory_space=pltpu.HBM)] * 2,
        out_specs=[pl.BlockSpec(memory_space=pltpu.HBM)] * 4,
        scratch_shapes=[
            pltpu.VMEM((3, tokens, heads_width), BF16),
            pltpu.VMEM((rows, width), BF16),
            pltpu.VMEM((rows, width), F32),
            dma((2, 3)),
            dma((STORES,)),
            dma((STORES,)),
        ],
        compiler_params=pltpu.CompilerParams(vmem_limit_bytes=58 * 1024 * 1024),
    )(*outs)
    return tuple(out[None] for out in stored[:3]) + (stored[3],)


def pick_body(mesh):
    if mesh.shape["seq"] == 2 and mesh.shape["dp"] == 4 and mesh.shape["fsdp"] == 4:
        return functools.partial(fused_body, mesh.shape["fsdp"])
    return body


def solution(mesh):
    return jax.shard_map(
        pick_body(mesh),
        mesh=mesh,
        in_specs=(
            P(("dp", "fsdp"), "seq", None),
            P(("dp", "fsdp"), "seq", None),
            P(("dp", "fsdp"), "seq", None),
            P(("dp", "fsdp"), "seq", None),
            P("fsdp", None),
        ),
        out_specs=(
            P(("dp", "fsdp"), "seq", None),
            P(("dp", "fsdp"), "seq", None),
            P(("dp", "fsdp"), "seq", None),
            P("fsdp", None),
        ),
        check_vma=False,
    )
```

```python
import functools

import jax
import jax.numpy as jnp
from jax import lax
from jax.experimental import pallas as pl
from jax.experimental.pallas import tpu as pltpu
from jax.sharding import PartitionSpec as P

DH = 128
LOG2E = 1.4426950408889634
CHUNKS = 4
STORES = 8
F32 = jnp.float32
BF16 = jnp.bfloat16


def head_backward(query_head, key_head, value_head, grad_head, block_rows):
    length = key_head.shape[0]
    score_scale = DH ** (-0.5)
    blocks = length // block_rows

    def visit(carry, block):
        key_acc, value_acc = carry
        begin = block * block_rows
        query_block = lax.dynamic_slice_in_dim(query_head, begin, block_rows, 0)
        grad_block = lax.dynamic_slice_in_dim(grad_head, begin, block_rows, 0)
        scores = (
            jnp.einsum("qd,kd->qk", query_block, key_head, preferred_element_type=jnp.float32)
            * score_scale
        )
        highest = jnp.max(scores, axis=1, keepdims=True)
        expanded = jnp.exp(scores - highest)
        weights = expanded / jnp.sum(expanded, axis=1, keepdims=True)
        weights_half = weights.astype(jnp.bfloat16)
        attended = jnp.einsum(
            "qk,kd->qd", weights_half, value_head, preferred_element_type=jnp.float32
        ).astype(jnp.bfloat16)
        grad_weights = jnp.einsum(
            "qd,kd->qk", grad_block, value_head, preferred_element_type=jnp.float32
        )
        row_delta = jnp.sum(weights * grad_weights, axis=1, keepdims=True)
        grad_scores = (weights * (grad_weights - row_delta)).astype(jnp.bfloat16)
        query_grad = (
            jnp.einsum("qk,kd->qd", grad_scores, key_head, preferred_element_type=jnp.float32)
            * score_scale
        ).astype(jnp.bfloat16)
        key_acc = key_acc + jnp.einsum(
            "qk,qd->kd", grad_scores, query_block, preferred_element_type=jnp.float32
        )
        value_acc = value_acc + jnp.einsum(
            "qk,qd->kd", weights_half, grad_block, preferred_element_type=jnp.float32
        )
        return ((key_acc, value_acc), (attended, query_grad))

    empty = jnp.zeros(key_head.shape, jnp.float32)
    finals, stacked = lax.scan(visit, (empty, empty), jnp.arange(blocks))
    attended = stacked[0].reshape(length, DH)
    query_grad = stacked[1].reshape(length, DH)
    key_grad = (finals[0] * score_scale).astype(jnp.bfloat16)
    value_grad = finals[1].astype(jnp.bfloat16)
    return (attended, query_grad, key_grad, value_grad)


def attend_heads(query_heads, key_heads, value_heads, grad_heads):
    length = query_heads.shape[1]
    per_device = query_heads.shape[2] // DH
    block_rows = min(512, length)
    gathered = [[], [], [], []]
    for head_index in range(per_device):
        lower = head_index * DH
        upper = lower + DH
        results = head_backward(
            query_heads[0, :, lower:upper],
            key_heads[0, :, lower:upper],
            value_heads[0, :, lower:upper],
            grad_heads[0, :, lower:upper],
            block_rows,
        )
        for position, result in enumerate(results):
            gathered[position].append(result)
    return tuple((jnp.concatenate(group, axis=1)[None] for group in gathered))


def body(queries, key_rows, value_rows, cotangent, out_weight):
    samples = lax.axis_size("dp") * lax.axis_size("fsdp")
    grad_out = jnp.einsum(
        "btd,rd->btr",
        cotangent,
        lax.all_gather(out_weight, "fsdp", axis=0, tiled=True),
        preferred_element_type=jnp.float32,
    ).astype(jnp.bfloat16)
    query_heads, key_heads, value_heads, grad_heads = (
        lax.all_to_all(queries, "seq", split_axis=2, concat_axis=1, tiled=True),
        lax.all_to_all(key_rows, "seq", split_axis=2, concat_axis=1, tiled=True),
        lax.all_to_all(value_rows, "seq", split_axis=2, concat_axis=1, tiled=True),
        lax.all_to_all(grad_out, "seq", split_axis=2, concat_axis=1, tiled=True),
    )
    head_results = attend_heads(query_heads, key_heads, value_heads, grad_heads)
    attended, query_grad, key_grad, value_grad = (
        lax.all_to_all(head_results[0], "seq", split_axis=1, concat_axis=2, tiled=True),
        lax.all_to_all(head_results[1], "seq", split_axis=1, concat_axis=2, tiled=True),
        lax.all_to_all(head_results[2], "seq", split_axis=1, concat_axis=2, tiled=True),
        lax.all_to_all(head_results[3], "seq", split_axis=1, concat_axis=2, tiled=True),
    )
    shares = lax.psum_scatter(
        jnp.einsum("btr,btd->rd", attended, cotangent, preferred_element_type=jnp.float32),
        ("fsdp", "seq"),
        scatter_dimension=0,
        tiled=True,
    )
    shares = lax.psum(shares.astype(jnp.bfloat16), "dp").astype(jnp.float32)
    total = lax.all_gather(shares.astype(jnp.bfloat16), "seq", axis=0, tiled=True).astype(
        shares.dtype
    )
    return (query_grad, key_grad, value_grad, total / samples)


def dot_nn(a, b):
    return lax.dot_general(a, b, (((1,), (0,)), ((), ())), preferred_element_type=F32)


def dot_nt(a, b):
    return lax.dot_general(a, b, (((1,), (1,)), ((), ())), preferred_element_type=F32)


def dot_tn(a, b):
    return lax.dot_general(a, b, (((0,), (0,)), ((), ())), preferred_element_type=F32)


def fused_kernel(
    nf,
    q_hbm,
    k_hbm,
    v_hbm,
    c_hbm,
    w_hbm,
    gr_ref,
    final,
    cot,
    qkv,
    go_out,
    go_in,
    at_out,
    at_in,
    probs,
    grads,
    w_ref,
    acc,
    y_out,
    y_in,
    x_out,
    x_in,
    d_out,
    d_in,
    w_sem,
    in_send,
    in_recv,
    cot_z,
    cot_fw,
    cot_sib,
    cot_x,
    cot_recv,
    go_send,
    go_recv,
    at_send,
    at_recv,
    out_send,
    out_recv,
    rs_send,
    rs_recv,
    ag_send,
    ag_recv,
    ds_send,
    ds_recv,
    dg_send,
    dg_recv,
    df_send,
    df_recv,
):
    tokens, width = c_hbm.shape
    rows = w_hbm.shape[0]
    part = width // CHUNKS
    core_rows = rows // 2
    half_rows = core_rows // 2
    group_heads = core_rows // DH
    length = 2 * tokens
    scale = DH ** (-0.5)
    dp = lax.axis_index("dp")
    f = lax.axis_index("fsdp")
    s = lax.axis_index("seq")
    core = dp % 2
    half = dp // 2
    twin = half * 2 + (1 - core)
    sibling = {"dp": twin}
    across = {"dp": (1 - half) * 2 + core}
    partner = {"seq": 1 - s}
    diagonal = {"dp": twin, "seq": 1 - s}
    native = core == s
    foreign = core != s
    inner = (f > 0) & (f < nf - 1)
    first = 1 + f % 2
    second = (2 + 3 * f) % 5
    third = 6 - f - first - second
    end = 3 * (f - 1)
    outer = jnp.logical_not(inner)
    corner = {"dp": (1 - half) * 2 + core, "seq": 1 - s}

    def remote(src, dst, send, recv, device):
        return pltpu.make_async_remote_copy(
            src_ref=src,
            dst_ref=dst,
            send_sem=send,
            recv_sem=recv,
            device_id=device,
            device_id_type=pl.DeviceIdType.MESH,
        )

    def wait_into(ref, sem):
        pltpu.make_async_copy(ref, ref, sem).wait()

    def head_cols(g, c):
        return pl.ds(pl.multiple_of(g * rows + c * core_rows, core_rows), core_rows)

    def chunk(k):
        return c_hbm.at[:, k * part : (k + 1) * part]

    def group_at(i):
        return (f + 1 + i) % nf

    def near_local(which, g):
        src = (q_hbm, k_hbm, v_hbm)[which]
        return pltpu.make_async_copy(
            src.at[:, head_cols(g, core)], qkv.at[which, g, s], in_recv.at[which, g, s]
        )

    def near_copy(which, g):
        src = (q_hbm, k_hbm, v_hbm)[which]
        return remote(
            src.at[:, head_cols(g, core)],
            qkv.at[which, g, s],
            in_send.at[0, which, g],
            in_recv.at[which, g, s],
            {"seq": core},
        )

    def far_copy(which, g):
        src = (q_hbm, k_hbm, v_hbm)[which]
        return remote(
            src.at[:, head_cols(g, 1 - core)],
            qkv.at[which, g, s],
            in_send.at[1, which, g],
            in_recv.at[which, g, s],
            {"dp": twin, "seq": core},
        )

    def own_local(k):
        return pltpu.make_async_copy(chunk(k), cot.at[f, core, k], cot_recv.at[f, core, k])

    def own_z(lane, k, src):
        return remote(
            src,
            cot.at[f, core, k],
            cot_z.at[lane, k],
            cot_recv.at[f, core, k],
            {"fsdp": (first, second)[lane]},
        )

    def to_sibling(j, k, src):
        return remote(src, cot.at[j, core, k], cot_sib.at[j, k], cot_recv.at[j, core, k], sibling)

    def cross(k):
        return remote(
            chunk(k), cot.at[f, 1 - core, k], cot_x.at[k], cot_recv.at[f, 1 - core, k], diagonal
        )

    def passed(i):
        return (3 - f) + i * (3 - 2 * f)

    def pass_on(i, k):
        j = passed(i)
        block = cot.at[j, core, k]
        return remote(block, block, cot_fw.at[i, k], cot_recv.at[j, core, k], {"fsdp": end})

    def go_copy(j):
        return remote(go_out.at[j], go_in.at[f], go_send.at[j], go_recv.at[f], {"fsdp": j})

    def at_copy(j):
        return remote(at_out.at[j], at_in.at[f], at_send.at[j], at_recv.at[f], {"fsdp": j})

    def home_local(g):
        return pltpu.make_async_copy(
            grads.at[g, s], gr_ref.at[:, :, head_cols(g, core)], out_recv.at[g, core]
        )

    def home_copy(g, t):
        return remote(
            grads.at[g, t],
            gr_ref.at[:, :, head_cols(g, core)],
            out_send.at[g, t],
            out_recv.at[g, core],
            {"dp": half * 2 + s, "seq": t},
        )

    w_load = pltpu.make_async_copy(
        w_hbm.at[pl.ds(pl.multiple_of(core * core_rows, core_rows), core_rows), :], w_ref, w_sem
    )

    @pl.when(native)
    def _():
        for i in range(nf):
            for which in range(3):
                near_local(which, group_at(i)).start()

    barrier = pltpu.get_barrier_semaphore()
    for device in (sibling, across, partner, diagonal, corner):
        pl.semaphore_signal(
            barrier, inc=1, device_id=device, device_id_type=pl.DeviceIdType.MESH
        )
    for step in range(1, nf):
        pl.semaphore_signal(
            barrier,
            inc=1,
            device_id={"fsdp": (f + step) % nf},
            device_id_type=pl.DeviceIdType.MESH,
        )
    pl.semaphore_wait(barrier, 5 + nf - 1)

    @pl.when(native)
    def _():
        for k in range(CHUNKS):
            own_z(0, k, chunk(k)).start()
            own_z(1, k, chunk(k)).start()
        for i in range(nf):
            for which in range(3):
                far_copy(which, group_at(i)).start()
        for k in range(CHUNKS):
            own_local(k).start()
            to_sibling(f, k, chunk(k)).start()

    @pl.when(foreign)
    def _():
        for i in range(nf):
            for which in range(3):
                near_copy(which, group_at(i)).start()
                far_copy(which, group_at(i)).start()
            cross(i).start()

    w_load.start()

    def head_of(which, g, inner_cols):
        return qkv[which, g, :, :, inner_cols].reshape(length, DH)

    def soften(i):
        g = group_at(i)
        for which in range(3):
            for t in range(2):
                wait_into(qkv.at[which, g, t], in_recv.at[which, g, t])
        for t in range(group_heads):
            cols = slice(t * DH, (t + 1) * DH)
            scores = dot_nt(head_of(0, g, cols), head_of(1, g, cols))
            highest = jnp.max(scores, axis=1, keepdims=True)
            expanded = jnp.exp2((scores - highest) * (scale * LOG2E))
            weights = expanded * (1.0 / jnp.sum(expanded, axis=1, keepdims=True))
            probs[g * group_heads + t] = weights
            at_out[g, :, cols] = dot_nn(weights.astype(BF16), head_of(2, g, cols)).astype(BF16)
        if i == nf - 1:
            at_in[f] = at_out[f]
        else:
            at_copy(g).start()

    def differentiate(g):
        for t in range(group_heads):
            cols = slice(t * DH, (t + 1) * DH)
            qh, kh, vh = (head_of(which, g, cols) for which in range(3))
            gh = go_in[g, :, cols]
            weights = probs[g * group_heads + t]
            grad_weights = dot_nt(gh, vh)
            delta = jnp.sum(weights * grad_weights, axis=1, keepdims=True)
            grad_scores = (weights * (grad_weights - delta)).astype(BF16)
            results = (
                dot_nn(grad_scores, kh) * scale,
                dot_tn(grad_scores, qh) * scale,
                dot_tn(weights.astype(BF16), gh),
            )
            for which, result in enumerate(results):
                grads[g, :, which, :, cols] = result.astype(BF16).reshape(2, tokens, DH)
        home_copy(g, 1 - s).start()

        @pl.when(native)
        def _():
            home_local(g).start()

        @pl.when(foreign)
        def _():
            home_copy(g, s).start()

    def project(j):
        total = None
        for k in range(CHUNKS):
            term = dot_nt(
                cot[j, :, k].reshape(length, part), w_ref[:, k * part : (k + 1) * part]
            )
            total = term if total is None else total + term
        return total.astype(BF16)

    def take(j, k):
        wait_into(cot.at[j, core, k], cot_recv.at[j, core, k])

    def take_other(j, k):
        wait_into(cot.at[j, 1 - core, k], cot_recv.at[j, 1 - core, k])

    def share(j, k):
        take(j, k)
        to_sibling(j, k, cot.at[j, core, k]).start()

    def urgent(k):
        @pl.when(inner)
        def _():
            for i in range(2):
                j = passed(i)
                take(j, k)
                pass_on(i, k).start()
                to_sibling(j, k, cot.at[j, core, k]).start()

    def pass_own(k):
        take(f, k)
        own_z(0, k, cot.at[f, core, k]).start()
        own_z(1, k, cot.at[f, core, k]).start()
        to_sibling(f, k, cot.at[f, core, k]).start()

    def for_native(*chunks):
        @pl.when(native)
        def _():
            for k in chunks:
                urgent(k)

    def for_foreign(*chunks):
        @pl.when(foreign)
        def _():
            for k in chunks:
                urgent(k)

    def for_own(k):
        @pl.when(foreign)
        def _():
            pass_own(k)

    for_native(0)
    soften(0)
    for_native(1)
    for_own(0)
    soften(1)
    for_native(2)
    for_own(1)
    soften(2)
    for_native(3)
    for_own(2)
    for_foreign(0)
    soften(3)
    for_own(3)

    @pl.when(native)
    def _():
        for k in range(CHUNKS):
            take(f, k)

    for k in range(CHUNKS):
        take_other(f, k)
    w_load.wait()
    go_in[f] = project(f)
    differentiate(f)

    def mine():
        return pl.ds(pl.multiple_of(half * half_rows, half_rows), half_rows)

    def theirs():
        return pl.ds(pl.multiple_of((1 - half) * half_rows, half_rows), half_rows)

    def reduce_copy(stage, c):
        src, dst = ((y_out, y_in), (x_out, x_in))[stage]
        device = (across, partner)[stage]
        return remote(src.at[c], dst.at[c], rs_send.at[stage, c], rs_recv.at[stage, c], device)

    def gather_copy(stage, c):
        which = half if stage < 2 else 1 - half
        base = core * core_rows + which * half_rows
        block = final.at[c, pl.ds(pl.multiple_of(base, half_rows), half_rows)]
        device = (across, sibling, sibling)[stage]
        return remote(block, block, ag_send.at[stage, c], ag_recv.at[stage, c], device)

    last = CHUNKS - 1

    def quarter_of(h, t):
        count = half_rows // 2
        return pl.ds(pl.multiple_of((h * 2 + t) * count, count), count)

    others = ((half, 1 - s, partner), (1 - half, s, across), (1 - half, 1 - s, corner))

    def direct_copy(i):
        h, t, device = others[i]
        return remote(d_out.at[quarter_of(h, t)], d_in.at[i], ds_send.at[i], ds_recv.at[i], device)

    def piece(c, h, t):
        base = core * core_rows + (h * 2 + t) * (half_rows // 2)
        return final.at[last, pl.ds(pl.multiple_of(base, half_rows // 2), half_rows // 2)]

    def spread_copy(i):
        block = piece(core, half, s)
        device = (partner, across, corner, sibling)[i]
        return remote(block, block, dg_send.at[i], dg_recv.at[i], device)

    def relay_copy(i):
        h, t, _ = others[i]
        block = piece(core, h, t)
        return remote(block, block, df_send.at[i], df_recv.at[i], sibling)

    def weight_term(c):
        if c == 0:
            for d in (first, second, third):
                wait_into(at_in.at[d], at_recv.at[d])
        at_all = at_in[...].reshape(nf * length, core_rows)
        acc[c] = dot_tn(at_all, cot[:, :, c].reshape(nf * length, part))
        if c < last:
            y_out[c] = acc[c, theirs()].astype(BF16)
            reduce_copy(0, c).start()
        else:
            d_out[...] = acc[c].astype(BF16)
            for i in (2, 1, 0):
                direct_copy(i).start()

    def reduce_direct(c):
        total = acc[last, quarter_of(half, s)]
        for i in range(3):
            direct_copy(i).wait_recv()
            total = total + d_in[i].astype(F32)
        piece(core, half, s)[...] = total.astype(BF16)
        for i in (2, 1, 0, 3):
            spread_copy(i).start()

    def gather_direct(c):
        for i in range(3):
            spread_copy(i).wait_recv()
            relay_copy(i).start()

    def gather_last(c):
        spread_copy(3).wait_recv()
        for i in range(3):
            relay_copy(i).wait_recv()

    def reduce_y(c):
        reduce_copy(0, c).wait_recv()
        x_out[c] = (acc[c, mine()] + y_in[c].astype(F32)).astype(BF16)
        reduce_copy(1, c).start()

    def reduce_x(c):
        reduce_copy(1, c).wait_recv()
        base = core * core_rows + half * half_rows
        final[c, pl.ds(pl.multiple_of(base, half_rows), half_rows)] = (
            x_out[c].astype(F32) + x_in[c].astype(F32)
        ).astype(BF16)
        gather_copy(0, c).start()
        gather_copy(1, c).start()

    def gather_y(c):
        gather_copy(0, c).wait_recv()
        gather_copy(2, c).start()

    def gather_core(c):
        gather_copy(1, c).wait_recv()
        gather_copy(2, c).wait_recv()

    def send_go(j):
        go_out[j] = project(j)
        go_copy(j).start()

    def take_go(j):
        wait_into(go_in.at[j], go_recv.at[j])
        differentiate(j)

    def arrive(j, k):
        share(j, k)
        take_other(j, k)

    def all_arrive(k):
        for j in (first, second, third):
            share(j, k)
        for j in (first, second, third):
            take_other(j, k)

    def end_arrives(k):
        arrive(second, k)

    def passed_arrive(k):
        if k > 0:
            for_foreign(k)
        take_other(first, k)
        take_other(third, k)

    def play(*steps):
        for action, argument in steps:
            action(argument)

    @pl.when(inner)
    def _():
        play(
            (end_arrives, 0),
            (passed_arrive, 0),
            (weight_term, 0),
            (end_arrives, 1),
            (passed_arrive, 1),
            (weight_term, 1),
            (end_arrives, 2),
            (end_arrives, 3),
            (send_go, second),
            (reduce_y, 0),
            (passed_arrive, 2),
            (weight_term, 2),
            (reduce_y, 1),
            (passed_arrive, 3),
            (weight_term, 3),
            (send_go, third),
            (send_go, first),
            (reduce_x, 0),
            (reduce_y, 2),
            (take_go, first),
            (reduce_x, 1),
            (gather_y, 0),
            (reduce_direct, last),
            (reduce_x, 2),
            (gather_y, 1),
            (gather_core, 0),
            (take_go, third),
            (gather_direct, last),
            (take_go, second),
            (gather_y, 2),
            (gather_core, 1),
            (gather_last, last),
            (gather_core, 2),
        )

    @pl.when(outer)
    def _():
        play(
            (all_arrive, 0),
            (weight_term, 0),
            (all_arrive, 1),
            (weight_term, 1),
            (reduce_y, 0),
            (take_go, first),
            (all_arrive, 2),
            (weight_term, 2),
            (reduce_y, 1),
            (reduce_x, 0),
            (all_arrive, 3),
            (weight_term, 3),
            (send_go, third),
            (send_go, second),
            (send_go, first),
            (reduce_y, 2),
            (reduce_x, 1),
            (gather_y, 0),
            (take_go, second),
            (reduce_direct, last),
            (gather_y, 1),
            (gather_core, 0),
            (take_go, third),
            (reduce_x, 2),
            (gather_direct, last),
            (gather_core, 1),
            (gather_y, 2),
            (gather_last, last),
            (gather_core, 2),
        )

    for g in range(nf):
        for c in range(2):
            wait_into(gr_ref.at[:, :, head_cols(g, c)], out_recv.at[g, c])
    for c in range(CHUNKS):
        if c == last:
            continue
        for stage in range(2):
            reduce_copy(stage, c).wait_send()
        for stage in range(3):
            gather_copy(stage, c).wait_send()
    for i in range(3):
        direct_copy(i).wait_send()
        relay_copy(i).wait_send()
    for i in range(4):
        spread_copy(i).wait_send()
    for j in (first, second, third):
        go_copy(j).wait_send()
        at_copy(j).wait_send()
    for g in range(nf):
        home_copy(g, 1 - s).wait_send()
        for which in range(3):
            far_copy(which, g).wait_send()
    for k in range(CHUNKS):
        own_z(0, k, cot.at[f, core, k]).wait_send()
        own_z(1, k, cot.at[f, core, k]).wait_send()
        for j in range(nf):
            to_sibling(j, k, cot.at[j, core, k]).wait_send()

    @pl.when(inner)
    def _():
        for k in range(CHUNKS):
            for i in range(2):
                pass_on(i, k).wait_send()

    @pl.when(foreign)
    def _():
        for g in range(nf):
            home_copy(g, s).wait_send()
            for which in range(3):
                near_copy(which, g).wait_send()
        for k in range(CHUNKS):
            cross(k).wait_send()


def store_kernel(factor, gr, wg, qg_out, kg_out, vg_out, wg_out, wide, sems, out_sems):
    count = wg.shape[1] // STORES
    part = wg.shape[2]
    copies = [
        pltpu.make_async_copy(gr.at[i], dst, sems.at[i])
        for i, dst in enumerate((qg_out, kg_out, vg_out))
    ]
    for i in range(STORES):
        block = slice(i * count, (i + 1) * count)
        for c in range(CHUNKS):
            wide[i, :, c * part : (c + 1) * part] = wg[c, block].astype(F32) * factor
        pltpu.make_async_copy(wide.at[i], wg_out.at[block], out_sems.at[i]).start()
        if i < 3:
            copies[i].start()
    for i in range(STORES):
        block = slice(i * count, (i + 1) * count)
        pltpu.make_async_copy(wide.at[i], wg_out.at[block], out_sems.at[i]).wait()
    for copy in copies:
        copy.wait()


def fused_body(nf, queries, key_rows, value_rows, cotangent, out_weight):
    samples = lax.axis_size("dp") * nf
    tokens, heads_width = queries.shape[1:]
    rows, width = out_weight.shape
    part = width // CHUNKS
    core_rows = rows // 2
    half_rows = core_rows // 2
    length = 2 * tokens
    heads = heads_width // DH // 2
    dma = pltpu.SemaphoreType.DMA
    outs = pl.pallas_call(
        functools.partial(fused_kernel, nf),
        out_shape=(
            pltpu.VMEM((3, tokens, heads_width), BF16),
            pltpu.VMEM((CHUNKS, rows, part), BF16),
        ),
        in_specs=[pl.BlockSpec(memory_space=pltpu.HBM)] * 5,
        out_specs=[pl.BlockSpec(memory_space=pltpu.VMEM)] * 2,
        scratch_shapes=[
            pltpu.VMEM((nf, 2, CHUNKS, tokens, part), BF16),
            pltpu.VMEM((3, nf, 2, tokens, core_rows), BF16),
            pltpu.VMEM((nf, length, core_rows), BF16),
            pltpu.VMEM((nf, length, core_rows), BF16),
            pltpu.VMEM((nf, length, core_rows), BF16),
            pltpu.VMEM((nf, length, core_rows), BF16),
            pltpu.VMEM((heads, length, length), F32),
            pltpu.VMEM((nf, 2, 3, tokens, core_rows), BF16),
            pltpu.VMEM((core_rows, width), BF16),
            pltpu.VMEM((CHUNKS, core_rows, part), F32),
            pltpu.VMEM((CHUNKS, half_rows, part), BF16),
            pltpu.VMEM((CHUNKS, half_rows, part), BF16),
            pltpu.VMEM((CHUNKS, half_rows, part), BF16),
            pltpu.VMEM((CHUNKS, half_rows, part), BF16),
            pltpu.VMEM((core_rows, part), BF16),
            pltpu.VMEM((3, half_rows // 2, part), BF16),
            dma,
            dma((2, 3, nf)),
            dma((3, nf, 2)),
            dma((2, CHUNKS)),
            dma((2, CHUNKS)),
            dma((nf, CHUNKS)),
            dma((CHUNKS,)),
            dma((nf, 2, CHUNKS)),
            dma((nf,)),
            dma((nf,)),
            dma((nf,)),
            dma((nf,)),
            dma((nf, 2)),
            dma((nf, 2)),
            dma((2, CHUNKS)),
            dma((2, CHUNKS)),
            dma((3, CHUNKS)),
            dma((3, CHUNKS)),
            dma((3,)),
            dma((3,)),
            dma((4,)),
            dma((4,)),
            dma((3,)),
            dma((3,)),
        ],
        compiler_params=pltpu.CompilerParams(
            collective_id=0, has_side_effects=True, vmem_limit_bytes=58 * 1024 * 1024
        ),
    )(queries[0], key_rows[0], value_rows[0], cotangent[0], out_weight)
    stored = pl.pallas_call(
        functools.partial(store_kernel, 1.0 / samples),
        out_shape=(jax.ShapeDtypeStruct((tokens, heads_width), BF16),) * 3
        + (jax.ShapeDtypeStruct((rows, width), F32),),
        in_specs=[pl.BlockSpec(memory_space=pltpu.VMEM)] * 2,
        out_specs=[pl.BlockSpec(memory_space=pltpu.HBM)] * 4,
        scratch_shapes=[
            pltpu.VMEM((STORES, rows // STORES, width), F32),
            dma((3,)),
            dma((STORES,)),
        ],
        compiler_params=pltpu.CompilerParams(vmem_limit_bytes=24 * 1024 * 1024),
    )(*outs)
    return tuple(out[None] for out in stored[:3]) + (stored[3],)


def pick_body(mesh):
    if mesh.shape["seq"] == 2 and mesh.shape["dp"] == 4 and mesh.shape["fsdp"] == 4:
        return functools.partial(fused_body, mesh.shape["fsdp"])
    return body


def solution(mesh):
    return jax.shard_map(
        pick_body(mesh),
        mesh=mesh,
        in_specs=(
            P(("dp", "fsdp"), "seq", None),
            P(("dp", "fsdp"), "seq", None),
            P(("dp", "fsdp"), "seq", None),
            P(("dp", "fsdp"), "seq", None),
            P("fsdp", None),
        ),
        out_specs=(
            P(("dp", "fsdp"), "seq", None),
            P(("dp", "fsdp"), "seq", None),
            P(("dp", "fsdp"), "seq", None),
            P("fsdp", None),
        ),
        check_vma=False,
    )
```

```python
import functools

import jax
import jax.numpy as jnp
from jax import lax
from jax.experimental import pallas as pl
from jax.experimental.pallas import tpu as pltpu
from jax.sharding import PartitionSpec as P

DH = 128
LOG2E = 1.4426950408889634
CHUNKS = 4
STORES = 8
F32 = jnp.float32
BF16 = jnp.bfloat16


def head_backward(query_head, key_head, value_head, grad_head, block_rows):
    length = key_head.shape[0]
    score_scale = DH ** (-0.5)
    blocks = length // block_rows

    def visit(carry, block):
        key_acc, value_acc = carry
        begin = block * block_rows
        query_block = lax.dynamic_slice_in_dim(query_head, begin, block_rows, 0)
        grad_block = lax.dynamic_slice_in_dim(grad_head, begin, block_rows, 0)
        scores = (
            jnp.einsum("qd,kd->qk", query_block, key_head, preferred_element_type=jnp.float32)
            * score_scale
        )
        highest = jnp.max(scores, axis=1, keepdims=True)
        expanded = jnp.exp(scores - highest)
        weights = expanded / jnp.sum(expanded, axis=1, keepdims=True)
        weights_half = weights.astype(jnp.bfloat16)
        attended = jnp.einsum(
            "qk,kd->qd", weights_half, value_head, preferred_element_type=jnp.float32
        ).astype(jnp.bfloat16)
        grad_weights = jnp.einsum(
            "qd,kd->qk", grad_block, value_head, preferred_element_type=jnp.float32
        )
        row_delta = jnp.sum(weights * grad_weights, axis=1, keepdims=True)
        grad_scores = (weights * (grad_weights - row_delta)).astype(jnp.bfloat16)
        query_grad = (
            jnp.einsum("qk,kd->qd", grad_scores, key_head, preferred_element_type=jnp.float32)
            * score_scale
        ).astype(jnp.bfloat16)
        key_acc = key_acc + jnp.einsum(
            "qk,qd->kd", grad_scores, query_block, preferred_element_type=jnp.float32
        )
        value_acc = value_acc + jnp.einsum(
            "qk,qd->kd", weights_half, grad_block, preferred_element_type=jnp.float32
        )
        return ((key_acc, value_acc), (attended, query_grad))

    empty = jnp.zeros(key_head.shape, jnp.float32)
    finals, stacked = lax.scan(visit, (empty, empty), jnp.arange(blocks))
    attended = stacked[0].reshape(length, DH)
    query_grad = stacked[1].reshape(length, DH)
    key_grad = (finals[0] * score_scale).astype(jnp.bfloat16)
    value_grad = finals[1].astype(jnp.bfloat16)
    return (attended, query_grad, key_grad, value_grad)


def attend_heads(query_heads, key_heads, value_heads, grad_heads):
    length = query_heads.shape[1]
    per_device = query_heads.shape[2] // DH
    block_rows = min(512, length)
    gathered = [[], [], [], []]
    for head_index in range(per_device):
        lower = head_index * DH
        upper = lower + DH
        results = head_backward(
            query_heads[0, :, lower:upper],
            key_heads[0, :, lower:upper],
            value_heads[0, :, lower:upper],
            grad_heads[0, :, lower:upper],
            block_rows,
        )
        for position, result in enumerate(results):
            gathered[position].append(result)
    return tuple((jnp.concatenate(group, axis=1)[None] for group in gathered))


def body(queries, key_rows, value_rows, cotangent, out_weight):
    samples = lax.axis_size("dp") * lax.axis_size("fsdp")
    grad_out = jnp.einsum(
        "btd,rd->btr",
        cotangent,
        lax.all_gather(out_weight, "fsdp", axis=0, tiled=True),
        preferred_element_type=jnp.float32,
    ).astype(jnp.bfloat16)
    query_heads, key_heads, value_heads, grad_heads = (
        lax.all_to_all(queries, "seq", split_axis=2, concat_axis=1, tiled=True),
        lax.all_to_all(key_rows, "seq", split_axis=2, concat_axis=1, tiled=True),
        lax.all_to_all(value_rows, "seq", split_axis=2, concat_axis=1, tiled=True),
        lax.all_to_all(grad_out, "seq", split_axis=2, concat_axis=1, tiled=True),
    )
    head_results = attend_heads(query_heads, key_heads, value_heads, grad_heads)
    attended, query_grad, key_grad, value_grad = (
        lax.all_to_all(head_results[0], "seq", split_axis=1, concat_axis=2, tiled=True),
        lax.all_to_all(head_results[1], "seq", split_axis=1, concat_axis=2, tiled=True),
        lax.all_to_all(head_results[2], "seq", split_axis=1, concat_axis=2, tiled=True),
        lax.all_to_all(head_results[3], "seq", split_axis=1, concat_axis=2, tiled=True),
    )
    shares = lax.psum_scatter(
        jnp.einsum("btr,btd->rd", attended, cotangent, preferred_element_type=jnp.float32),
        ("fsdp", "seq"),
        scatter_dimension=0,
        tiled=True,
    )
    shares = lax.psum(shares.astype(jnp.bfloat16), "dp").astype(jnp.float32)
    total = lax.all_gather(shares.astype(jnp.bfloat16), "seq", axis=0, tiled=True).astype(
        shares.dtype
    )
    return (query_grad, key_grad, value_grad, total / samples)


def dot_nn(a, b):
    return lax.dot_general(a, b, (((1,), (0,)), ((), ())), preferred_element_type=F32)


def dot_nt(a, b):
    return lax.dot_general(a, b, (((1,), (1,)), ((), ())), preferred_element_type=F32)


def dot_tn(a, b):
    return lax.dot_general(a, b, (((0,), (0,)), ((), ())), preferred_element_type=F32)


def fused_kernel(
    nf,
    q_hbm,
    k_hbm,
    v_hbm,
    c_hbm,
    w_hbm,
    gr_ref,
    final,
    cot,
    qkv,
    go_out,
    go_in,
    at_out,
    at_in,
    probs,
    grads,
    w_ref,
    acc,
    y_out,
    y_in,
    x_out,
    x_in,
    d_out,
    d_in,
    w_sem,
    in_send,
    in_recv,
    cot_z,
    cot_fw,
    cot_sib,
    cot_x,
    cot_recv,
    go_send,
    go_recv,
    at_send,
    at_recv,
    out_send,
    out_recv,
    rs_send,
    rs_recv,
    ag_send,
    ag_recv,
    ds_send,
    ds_recv,
    dg_send,
    dg_recv,
    df_send,
    df_recv,
):
    tokens, width = c_hbm.shape
    rows = w_hbm.shape[0]
    part = width // CHUNKS
    core_rows = rows // 2
    half_rows = core_rows // 2
    group_heads = core_rows // DH
    length = 2 * tokens
    scale = DH ** (-0.5)
    dp = lax.axis_index("dp")
    f = lax.axis_index("fsdp")
    s = lax.axis_index("seq")
    core = dp % 2
    half = dp // 2
    twin = half * 2 + (1 - core)
    sibling = {"dp": twin}
    across = {"dp": (1 - half) * 2 + core}
    partner = {"seq": 1 - s}
    diagonal = {"dp": twin, "seq": 1 - s}
    native = core == s
    foreign = core != s
    inner = (f > 0) & (f < nf - 1)
    first = 1 + f % 2
    second = (2 + 3 * f) % 5
    third = 6 - f - first - second
    end = 3 * (f - 1)
    outer = jnp.logical_not(inner)
    corner = {"dp": (1 - half) * 2 + core, "seq": 1 - s}

    def remote(src, dst, send, recv, device):
        return pltpu.make_async_remote_copy(
            src_ref=src,
            dst_ref=dst,
            send_sem=send,
            recv_sem=recv,
            device_id=device,
            device_id_type=pl.DeviceIdType.MESH,
        )

    def wait_into(ref, sem):
        pltpu.make_async_copy(ref, ref, sem).wait()

    def head_cols(g, c):
        return pl.ds(pl.multiple_of(g * rows + c * core_rows, core_rows), core_rows)

    def chunk(k):
        return c_hbm.at[:, k * part : (k + 1) * part]

    def group_at(i):
        return (f + 1 + i) % nf

    def near_local(which, g):
        src = (q_hbm, k_hbm, v_hbm)[which]
        return pltpu.make_async_copy(
            src.at[:, head_cols(g, core)], qkv.at[which, g, s], in_recv.at[which, g, s]
        )

    def near_copy(which, g):
        src = (q_hbm, k_hbm, v_hbm)[which]
        return remote(
            src.at[:, head_cols(g, core)],
            qkv.at[which, g, s],
            in_send.at[0, which, g],
            in_recv.at[which, g, s],
            {"seq": core},
        )

    def far_copy(which, g):
        src = (q_hbm, k_hbm, v_hbm)[which]
        return remote(
            src.at[:, head_cols(g, 1 - core)],
            qkv.at[which, g, s],
            in_send.at[1, which, g],
            in_recv.at[which, g, s],
            {"dp": twin, "seq": core},
        )

    def own_local(k):
        return pltpu.make_async_copy(chunk(k), cot.at[f, core, k], cot_recv.at[f, core, k])

    def own_z(lane, k, src):
        return remote(
            src,
            cot.at[f, core, k],
            cot_z.at[lane, k],
            cot_recv.at[f, core, k],
            {"fsdp": (first, second)[lane]},
        )

    def to_sibling(j, k, src):
        return remote(src, cot.at[j, core, k], cot_sib.at[j, k], cot_recv.at[j, core, k], sibling)

    def cross(k):
        return remote(
            chunk(k), cot.at[f, 1 - core, k], cot_x.at[k], cot_recv.at[f, 1 - core, k], diagonal
        )

    def passed(i):
        return (3 - f) + i * (3 - 2 * f)

    def pass_on(i, k):
        j = passed(i)
        block = cot.at[j, core, k]
        return remote(block, block, cot_fw.at[i, k], cot_recv.at[j, core, k], {"fsdp": end})

    def go_copy(j):
        return remote(go_out.at[j], go_in.at[f], go_send.at[j], go_recv.at[f], {"fsdp": j})

    def at_copy(j):
        return remote(at_out.at[j], at_in.at[f], at_send.at[j], at_recv.at[f], {"fsdp": j})

    def home_local(g):
        return pltpu.make_async_copy(
            grads.at[g, s], gr_ref.at[:, :, head_cols(g, core)], out_recv.at[g, core]
        )

    def home_copy(g, t):
        return remote(
            grads.at[g, t],
            gr_ref.at[:, :, head_cols(g, core)],
            out_send.at[g, t],
            out_recv.at[g, core],
            {"dp": half * 2 + s, "seq": t},
        )

    w_load = pltpu.make_async_copy(
        w_hbm.at[pl.ds(pl.multiple_of(core * core_rows, core_rows), core_rows), :], w_ref, w_sem
    )

    @pl.when(native)
    def _():
        for i in range(nf):
            for which in range(3):
                near_local(which, group_at(i)).start()

    barrier = pltpu.get_barrier_semaphore()
    for device in (sibling, across, partner, diagonal, corner):
        pl.semaphore_signal(
            barrier, inc=1, device_id=device, device_id_type=pl.DeviceIdType.MESH
        )
    for step in range(1, nf):
        pl.semaphore_signal(
            barrier,
            inc=1,
            device_id={"fsdp": (f + step) % nf},
            device_id_type=pl.DeviceIdType.MESH,
        )
    pl.semaphore_wait(barrier, 5 + nf - 1)

    @pl.when(native)
    def _():
        for k in range(CHUNKS):
            own_z(0, k, chunk(k)).start()
            own_z(1, k, chunk(k)).start()
        for i in range(nf):
            for which in range(3):
                far_copy(which, group_at(i)).start()
        for k in range(CHUNKS):
            own_local(k).start()
            to_sibling(f, k, chunk(k)).start()

    @pl.when(foreign)
    def _():
        for i in range(nf):
            for which in range(3):
                near_copy(which, group_at(i)).start()
                far_copy(which, group_at(i)).start()
            cross(i).start()

    w_load.start()

    def head_of(which, g, inner_cols):
        return qkv[which, g, :, :, inner_cols].reshape(length, DH)

    def soften(i):
        g = group_at(i)
        for which in range(3):
            for t in range(2):
                wait_into(qkv.at[which, g, t], in_recv.at[which, g, t])
        for t in range(group_heads):
            cols = slice(t * DH, (t + 1) * DH)
            scores = dot_nt(head_of(0, g, cols), head_of(1, g, cols))
            highest = jnp.max(scores, axis=1, keepdims=True)
            expanded = jnp.exp2((scores - highest) * (scale * LOG2E))
            weights = expanded * (1.0 / jnp.sum(expanded, axis=1, keepdims=True))
            probs[g * group_heads + t] = weights
            at_out[g, :, cols] = dot_nn(weights.astype(BF16), head_of(2, g, cols)).astype(BF16)
        if i == nf - 1:
            at_in[f] = at_out[f]
        else:
            at_copy(g).start()

    def differentiate(g):
        for t in range(group_heads):
            cols = slice(t * DH, (t + 1) * DH)
            qh, kh, vh = (head_of(which, g, cols) for which in range(3))
            gh = go_in[g, :, cols]
            weights = probs[g * group_heads + t]
            grad_weights = dot_nt(gh, vh)
            delta = jnp.sum(weights * grad_weights, axis=1, keepdims=True)
            grad_scores = (weights * (grad_weights - delta)).astype(BF16)
            results = (
                dot_nn(grad_scores, kh) * scale,
                dot_tn(grad_scores, qh) * scale,
                dot_tn(weights.astype(BF16), gh),
            )
            for which, result in enumerate(results):
                grads[g, :, which, :, cols] = result.astype(BF16).reshape(2, tokens, DH)
        home_copy(g, 1 - s).start()

        @pl.when(native)
        def _():
            home_local(g).start()

        @pl.when(foreign)
        def _():
            home_copy(g, s).start()

    def project(j):
        total = None
        for k in range(CHUNKS):
            term = dot_nt(
                cot[j, :, k].reshape(length, part), w_ref[:, k * part : (k + 1) * part]
            )
            total = term if total is None else total + term
        return total.astype(BF16)

    def take(j, k):
        wait_into(cot.at[j, core, k], cot_recv.at[j, core, k])

    def take_other(j, k):
        wait_into(cot.at[j, 1 - core, k], cot_recv.at[j, 1 - core, k])

    def share(j, k):
        take(j, k)
        to_sibling(j, k, cot.at[j, core, k]).start()

    def urgent(k):
        @pl.when(inner)
        def _():
            for i in range(2):
                j = passed(i)
                take(j, k)
                pass_on(i, k).start()
                to_sibling(j, k, cot.at[j, core, k]).start()

    def pass_own(k):
        take(f, k)
        own_z(0, k, cot.at[f, core, k]).start()
        own_z(1, k, cot.at[f, core, k]).start()
        to_sibling(f, k, cot.at[f, core, k]).start()

    def for_native(*chunks):
        @pl.when(native)
        def _():
            for k in chunks:
                urgent(k)

    def for_foreign(*chunks):
        @pl.when(foreign)
        def _():
            for k in chunks:
                urgent(k)

    def for_own(k):
        @pl.when(foreign)
        def _():
            pass_own(k)

    for_native(0)
    soften(0)
    for_native(1)
    for_own(0)
    soften(1)
    for_native(2)
    for_own(1)
    soften(2)
    for_native(3)
    for_own(2)
    for_foreign(0)
    soften(3)
    for_own(3)

    @pl.when(native)
    def _():
        for k in range(CHUNKS):
            take(f, k)

    for k in range(CHUNKS):
        take_other(f, k)
    w_load.wait()
    go_in[f] = project(f)
    differentiate(f)

    def mine():
        return pl.ds(pl.multiple_of(half * half_rows, half_rows), half_rows)

    def theirs():
        return pl.ds(pl.multiple_of((1 - half) * half_rows, half_rows), half_rows)

    def reduce_copy(stage, c):
        src, dst = ((y_out, y_in), (x_out, x_in))[stage]
        device = (across, partner)[stage]
        return remote(src.at[c], dst.at[c], rs_send.at[stage, c], rs_recv.at[stage, c], device)

    def gather_copy(stage, c):
        which = half if stage < 2 else 1 - half
        base = core * core_rows + which * half_rows
        block = final.at[c, pl.ds(pl.multiple_of(base, half_rows), half_rows)]
        device = (across, sibling, sibling)[stage]
        return remote(block, block, ag_send.at[stage, c], ag_recv.at[stage, c], device)

    last = CHUNKS - 1

    def quarter_of(h, t):
        count = half_rows // 2
        return pl.ds(pl.multiple_of((h * 2 + t) * count, count), count)

    others = ((half, 1 - s, partner), (1 - half, s, across), (1 - half, 1 - s, corner))

    def direct_copy(i):
        h, t, device = others[i]
        return remote(d_out.at[quarter_of(h, t)], d_in.at[i], ds_send.at[i], ds_recv.at[i], device)

    def piece(c, h, t):
        base = core * core_rows + (h * 2 + t) * (half_rows // 2)
        return final.at[last, pl.ds(pl.multiple_of(base, half_rows // 2), half_rows // 2)]

    def spread_copy(i):
        block = piece(core, half, s)
        device = (partner, across, corner, sibling)[i]
        return remote(block, block, dg_send.at[i], dg_recv.at[i], device)

    def relay_copy(i):
        h, t, _ = others[i]
        block = piece(core, h, t)
        return remote(block, block, df_send.at[i], df_recv.at[i], sibling)

    def weight_term(c):
        if c == 0:
            for d in (first, second, third):
                wait_into(at_in.at[d], at_recv.at[d])
        at_all = at_in[...].reshape(nf * length, core_rows)
        acc[c] = dot_tn(at_all, cot[:, :, c].reshape(nf * length, part))
        if c < last:
            y_out[c] = acc[c, theirs()].astype(BF16)
            reduce_copy(0, c).start()
        else:
            d_out[...] = acc[c].astype(BF16)
            for i in (2, 1, 0):
                direct_copy(i).start()

    def reduce_direct(c):
        total = acc[last, quarter_of(half, s)]
        for i in range(3):
            direct_copy(i).wait_recv()
            total = total + d_in[i].astype(F32)
        piece(core, half, s)[...] = total.astype(BF16)
        for i in (2, 1, 0, 3):
            spread_copy(i).start()

    def gather_direct(c):
        for i in range(3):
            spread_copy(i).wait_recv()
            relay_copy(i).start()

    def gather_last(c):
        spread_copy(3).wait_recv()
        for i in range(3):
            relay_copy(i).wait_recv()

    def reduce_y(c):
        reduce_copy(0, c).wait_recv()
        x_out[c] = (acc[c, mine()] + y_in[c].astype(F32)).astype(BF16)
        reduce_copy(1, c).start()

    def reduce_x(c):
        reduce_copy(1, c).wait_recv()
        base = core * core_rows + half * half_rows
        final[c, pl.ds(pl.multiple_of(base, half_rows), half_rows)] = (
            x_out[c].astype(F32) + x_in[c].astype(F32)
        ).astype(BF16)
        gather_copy(0, c).start()
        gather_copy(1, c).start()

    def gather_y(c):
        gather_copy(0, c).wait_recv()
        gather_copy(2, c).start()

    def gather_core(c):
        gather_copy(1, c).wait_recv()
        gather_copy(2, c).wait_recv()

    def send_go(j):
        go_out[j] = project(j)
        go_copy(j).start()

    def take_go(j):
        wait_into(go_in.at[j], go_recv.at[j])
        differentiate(j)

    def arrive(j, k):
        share(j, k)
        take_other(j, k)

    def all_arrive(k):
        for j in (first, second, third):
            share(j, k)
        for j in (first, second, third):
            take_other(j, k)

    def end_arrives(k):
        arrive(second, k)

    def passed_arrive(k):
        if k > 0:
            for_foreign(k)
        take_other(first, k)
        take_other(third, k)

    def settle(c):
        for g in range(nf):
            for which in range(3):
                far_copy(which, g).wait_send()
        for j in (first, second, third):
            at_copy(j).wait_send()
        for k in range(CHUNKS):
            own_z(0, k, cot.at[f, core, k]).wait_send()
            own_z(1, k, cot.at[f, core, k]).wait_send()
            to_sibling(f, k, cot.at[f, core, k]).wait_send()

        @pl.when(foreign)
        def _():
            for g in range(nf):
                for which in range(3):
                    near_copy(which, g).wait_send()
            for k in range(CHUNKS):
                cross(k).wait_send()

    def play(*steps):
        for action, argument in steps:
            action(argument)

    @pl.when(inner)
    def _():
        play(
            (end_arrives, 0),
            (passed_arrive, 0),
            (weight_term, 0),
            (end_arrives, 1),
            (passed_arrive, 1),
            (weight_term, 1),
            (end_arrives, 2),
            (end_arrives, 3),
            (send_go, second),
            (reduce_y, 0),
            (passed_arrive, 2),
            (weight_term, 2),
            (reduce_y, 1),
            (passed_arrive, 3),
            (weight_term, 3),
            (send_go, third),
            (send_go, first),
            (reduce_y, 2),
            (reduce_x, 0),
            (reduce_x, 1),
            (reduce_direct, last),
            (reduce_x, 2),
            (settle, 0),
            (take_go, first),
            (gather_direct, last),
            (gather_y, 0),
            (gather_core, 0),
            (gather_y, 1),
            (gather_core, 1),
            (gather_last, last),
            (gather_y, 2),
            (gather_core, 2),
            (take_go, second),
            (take_go, third),
        )

    @pl.when(outer)
    def _():
        play(
            (all_arrive, 0),
            (weight_term, 0),
            (all_arrive, 1),
            (weight_term, 1),
            (reduce_y, 0),
            (take_go, first),
            (all_arrive, 2),
            (weight_term, 2),
            (reduce_y, 1),
            (reduce_x, 0),
            (settle, 0),
            (all_arrive, 3),
            (weight_term, 3),
            (send_go, first),
            (send_go, second),
            (send_go, third),
            (reduce_y, 2),
            (reduce_x, 1),
            (take_go, second),
            (reduce_direct, last),
            (reduce_x, 2),
            (take_go, third),
            (gather_direct, last),
            (gather_y, 0),
            (gather_core, 0),
            (gather_y, 1),
            (gather_core, 1),
            (gather_last, last),
            (gather_y, 2),
            (gather_core, 2),
        )

    for g in range(nf):
        for c in range(2):
            wait_into(gr_ref.at[:, :, head_cols(g, c)], out_recv.at[g, c])
    for c in range(CHUNKS):
        if c == last:
            continue
        for stage in range(2):
            reduce_copy(stage, c).wait_send()
        for stage in range(3):
            gather_copy(stage, c).wait_send()
    for i in range(3):
        direct_copy(i).wait_send()
        relay_copy(i).wait_send()
    for i in range(4):
        spread_copy(i).wait_send()
    for j in (first, second, third):
        go_copy(j).wait_send()
    for g in range(nf):
        home_copy(g, 1 - s).wait_send()
    for k in range(CHUNKS):
        for j in (first, second, third):
            to_sibling(j, k, cot.at[j, core, k]).wait_send()

    @pl.when(inner)
    def _():
        for k in range(CHUNKS):
            for i in range(2):
                pass_on(i, k).wait_send()

    @pl.when(foreign)
    def _():
        for g in range(nf):
            home_copy(g, s).wait_send()


def store_kernel(factor, gr, wg, qg_out, kg_out, vg_out, wg_out, wide, sems, out_sems):
    count = wg.shape[1] // STORES
    part = wg.shape[2]
    copies = [
        pltpu.make_async_copy(gr.at[i], dst, sems.at[i])
        for i, dst in enumerate((qg_out, kg_out, vg_out))
    ]
    for i in range(STORES):
        block = slice(i * count, (i + 1) * count)
        for c in range(CHUNKS):
            wide[i, :, c * part : (c + 1) * part] = wg[c, block].astype(F32) * factor
        pltpu.make_async_copy(wide.at[i], wg_out.at[block], out_sems.at[i]).start()
        if i < 3:
            copies[i].start()
    for i in range(STORES):
        block = slice(i * count, (i + 1) * count)
        pltpu.make_async_copy(wide.at[i], wg_out.at[block], out_sems.at[i]).wait()
    for copy in copies:
        copy.wait()


def fused_body(nf, queries, key_rows, value_rows, cotangent, out_weight):
    samples = lax.axis_size("dp") * nf
    tokens, heads_width = queries.shape[1:]
    rows, width = out_weight.shape
    part = width // CHUNKS
    core_rows = rows // 2
    half_rows = core_rows // 2
    length = 2 * tokens
    heads = heads_width // DH // 2
    dma = pltpu.SemaphoreType.DMA
    outs = pl.pallas_call(
        functools.partial(fused_kernel, nf),
        out_shape=(
            pltpu.VMEM((3, tokens, heads_width), BF16),
            pltpu.VMEM((CHUNKS, rows, part), BF16),
        ),
        in_specs=[pl.BlockSpec(memory_space=pltpu.HBM)] * 5,
        out_specs=[pl.BlockSpec(memory_space=pltpu.VMEM)] * 2,
        scratch_shapes=[
            pltpu.VMEM((nf, 2, CHUNKS, tokens, part), BF16),
            pltpu.VMEM((3, nf, 2, tokens, core_rows), BF16),
            pltpu.VMEM((nf, length, core_rows), BF16),
            pltpu.VMEM((nf, length, core_rows), BF16),
            pltpu.VMEM((nf, length, core_rows), BF16),
            pltpu.VMEM((nf, length, core_rows), BF16),
            pltpu.VMEM((heads, length, length), F32),
            pltpu.VMEM((nf, 2, 3, tokens, core_rows), BF16),
            pltpu.VMEM((core_rows, width), BF16),
            pltpu.VMEM((CHUNKS, core_rows, part), F32),
            pltpu.VMEM((CHUNKS, half_rows, part), BF16),
            pltpu.VMEM((CHUNKS, half_rows, part), BF16),
            pltpu.VMEM((CHUNKS, half_rows, part), BF16),
            pltpu.VMEM((CHUNKS, half_rows, part), BF16),
            pltpu.VMEM((core_rows, part), BF16),
            pltpu.VMEM((3, half_rows // 2, part), BF16),
            dma,
            dma((2, 3, nf)),
            dma((3, nf, 2)),
            dma((2, CHUNKS)),
            dma((2, CHUNKS)),
            dma((nf, CHUNKS)),
            dma((CHUNKS,)),
            dma((nf, 2, CHUNKS)),
            dma((nf,)),
            dma((nf,)),
            dma((nf,)),
            dma((nf,)),
            dma((nf, 2)),
            dma((nf, 2)),
            dma((2, CHUNKS)),
            dma((2, CHUNKS)),
            dma((3, CHUNKS)),
            dma((3, CHUNKS)),
            dma((3,)),
            dma((3,)),
            dma((4,)),
            dma((4,)),
            dma((3,)),
            dma((3,)),
        ],
        compiler_params=pltpu.CompilerParams(
            collective_id=0, has_side_effects=True, vmem_limit_bytes=58 * 1024 * 1024
        ),
    )(queries[0], key_rows[0], value_rows[0], cotangent[0], out_weight)
    stored = pl.pallas_call(
        functools.partial(store_kernel, 1.0 / samples),
        out_shape=(jax.ShapeDtypeStruct((tokens, heads_width), BF16),) * 3
        + (jax.ShapeDtypeStruct((rows, width), F32),),
        in_specs=[pl.BlockSpec(memory_space=pltpu.VMEM)] * 2,
        out_specs=[pl.BlockSpec(memory_space=pltpu.HBM)] * 4,
        scratch_shapes=[
            pltpu.VMEM((STORES, rows // STORES, width), F32),
            dma((3,)),
            dma((STORES,)),
        ],
        compiler_params=pltpu.CompilerParams(vmem_limit_bytes=24 * 1024 * 1024),
    )(*outs)
    return tuple(out[None] for out in stored[:3]) + (stored[3],)


def pick_body(mesh):
    if mesh.shape["seq"] == 2 and mesh.shape["dp"] == 4 and mesh.shape["fsdp"] == 4:
        return functools.partial(fused_body, mesh.shape["fsdp"])
    return body


def solution(mesh):
    return jax.shard_map(
        pick_body(mesh),
        mesh=mesh,
        in_specs=(
            P(("dp", "fsdp"), "seq", None),
            P(("dp", "fsdp"), "seq", None),
            P(("dp", "fsdp"), "seq", None),
            P(("dp", "fsdp"), "seq", None),
            P("fsdp", None),
        ),
        out_specs=(
            P(("dp", "fsdp"), "seq", None),
            P(("dp", "fsdp"), "seq", None),
            P(("dp", "fsdp"), "seq", None),
            P("fsdp", None),
        ),
        check_vma=False,
    )
```

```python
import functools

import jax
import jax.numpy as jnp
from jax import lax
from jax.experimental import pallas as pl
from jax.experimental.pallas import tpu as pltpu
from jax.sharding import PartitionSpec as P

DH = 128
LOG2E = 1.4426950408889634
SHARES = (5, 4, 4, 3)
CHUNKS = len(SHARES)
STORES = 8
F32 = jnp.float32
BF16 = jnp.bfloat16


def head_backward(query_head, key_head, value_head, grad_head, block_rows):
    length = key_head.shape[0]
    score_scale = DH ** (-0.5)
    blocks = length // block_rows

    def visit(carry, block):
        key_acc, value_acc = carry
        begin = block * block_rows
        query_block = lax.dynamic_slice_in_dim(query_head, begin, block_rows, 0)
        grad_block = lax.dynamic_slice_in_dim(grad_head, begin, block_rows, 0)
        scores = (
            jnp.einsum("qd,kd->qk", query_block, key_head, preferred_element_type=jnp.float32)
            * score_scale
        )
        highest = jnp.max(scores, axis=1, keepdims=True)
        expanded = jnp.exp(scores - highest)
        weights = expanded / jnp.sum(expanded, axis=1, keepdims=True)
        weights_half = weights.astype(jnp.bfloat16)
        attended = jnp.einsum(
            "qk,kd->qd", weights_half, value_head, preferred_element_type=jnp.float32
        ).astype(jnp.bfloat16)
        grad_weights = jnp.einsum(
            "qd,kd->qk", grad_block, value_head, preferred_element_type=jnp.float32
        )
        row_delta = jnp.sum(weights * grad_weights, axis=1, keepdims=True)
        grad_scores = (weights * (grad_weights - row_delta)).astype(jnp.bfloat16)
        query_grad = (
            jnp.einsum("qk,kd->qd", grad_scores, key_head, preferred_element_type=jnp.float32)
            * score_scale
        ).astype(jnp.bfloat16)
        key_acc = key_acc + jnp.einsum(
            "qk,qd->kd", grad_scores, query_block, preferred_element_type=jnp.float32
        )
        value_acc = value_acc + jnp.einsum(
            "qk,qd->kd", weights_half, grad_block, preferred_element_type=jnp.float32
        )
        return ((key_acc, value_acc), (attended, query_grad))

    empty = jnp.zeros(key_head.shape, jnp.float32)
    finals, stacked = lax.scan(visit, (empty, empty), jnp.arange(blocks))
    attended = stacked[0].reshape(length, DH)
    query_grad = stacked[1].reshape(length, DH)
    key_grad = (finals[0] * score_scale).astype(jnp.bfloat16)
    value_grad = finals[1].astype(jnp.bfloat16)
    return (attended, query_grad, key_grad, value_grad)


def attend_heads(query_heads, key_heads, value_heads, grad_heads):
    length = query_heads.shape[1]
    per_device = query_heads.shape[2] // DH
    block_rows = min(512, length)
    gathered = [[], [], [], []]
    for head_index in range(per_device):
        lower = head_index * DH
        upper = lower + DH
        results = head_backward(
            query_heads[0, :, lower:upper],
            key_heads[0, :, lower:upper],
            value_heads[0, :, lower:upper],
            grad_heads[0, :, lower:upper],
            block_rows,
        )
        for position, result in enumerate(results):
            gathered[position].append(result)
    return tuple((jnp.concatenate(group, axis=1)[None] for group in gathered))


def body(queries, key_rows, value_rows, cotangent, out_weight):
    samples = lax.axis_size("dp") * lax.axis_size("fsdp")
    grad_out = jnp.einsum(
        "btd,rd->btr",
        cotangent,
        lax.all_gather(out_weight, "fsdp", axis=0, tiled=True),
        preferred_element_type=jnp.float32,
    ).astype(jnp.bfloat16)
    query_heads, key_heads, value_heads, grad_heads = (
        lax.all_to_all(queries, "seq", split_axis=2, concat_axis=1, tiled=True),
        lax.all_to_all(key_rows, "seq", split_axis=2, concat_axis=1, tiled=True),
        lax.all_to_all(value_rows, "seq", split_axis=2, concat_axis=1, tiled=True),
        lax.all_to_all(grad_out, "seq", split_axis=2, concat_axis=1, tiled=True),
    )
    head_results = attend_heads(query_heads, key_heads, value_heads, grad_heads)
    attended, query_grad, key_grad, value_grad = (
        lax.all_to_all(head_results[0], "seq", split_axis=1, concat_axis=2, tiled=True),
        lax.all_to_all(head_results[1], "seq", split_axis=1, concat_axis=2, tiled=True),
        lax.all_to_all(head_results[2], "seq", split_axis=1, concat_axis=2, tiled=True),
        lax.all_to_all(head_results[3], "seq", split_axis=1, concat_axis=2, tiled=True),
    )
    shares = lax.psum_scatter(
        jnp.einsum("btr,btd->rd", attended, cotangent, preferred_element_type=jnp.float32),
        ("fsdp", "seq"),
        scatter_dimension=0,
        tiled=True,
    )
    shares = lax.psum(shares.astype(jnp.bfloat16), "dp").astype(jnp.float32)
    total = lax.all_gather(shares.astype(jnp.bfloat16), "seq", axis=0, tiled=True).astype(
        shares.dtype
    )
    return (query_grad, key_grad, value_grad, total / samples)


def dot_nn(a, b):
    return lax.dot_general(a, b, (((1,), (0,)), ((), ())), preferred_element_type=F32)


def dot_nt(a, b):
    return lax.dot_general(a, b, (((1,), (1,)), ((), ())), preferred_element_type=F32)


def dot_tn(a, b):
    return lax.dot_general(a, b, (((0,), (0,)), ((), ())), preferred_element_type=F32)


def chunk_widths(width):
    unit = width // sum(SHARES)
    widths = [share * unit for share in SHARES]
    return widths, [sum(widths[:k]) for k in range(CHUNKS)]


def fused_kernel(
    nf,
    q_hbm,
    k_hbm,
    v_hbm,
    c_hbm,
    w_hbm,
    gr_ref,
    final,
    cot,
    qkv,
    go_out,
    go_in,
    at_out,
    at_in,
    probs,
    grads,
    w_ref,
    acc,
    y_out,
    y_in,
    x_out,
    x_in,
    d_out,
    d_in,
    w_sem,
    in_send,
    in_recv,
    cot_z,
    cot_fw,
    cot_sib,
    cot_x,
    cot_recv,
    go_send,
    go_recv,
    at_send,
    at_recv,
    out_send,
    out_recv,
    rs_send,
    rs_recv,
    ag_send,
    ag_recv,
    ds_send,
    ds_recv,
    dg_send,
    dg_recv,
    df_send,
    df_recv,
):
    tokens, width = c_hbm.shape
    rows = w_hbm.shape[0]
    widths, starts = chunk_widths(width)
    core_rows = rows // 2
    half_rows = core_rows // 2
    group_heads = core_rows // DH
    length = 2 * tokens
    scale = DH ** (-0.5)
    dp = lax.axis_index("dp")
    f = lax.axis_index("fsdp")
    s = lax.axis_index("seq")
    core = dp % 2
    half = dp // 2
    twin = half * 2 + (1 - core)
    sibling = {"dp": twin}
    across = {"dp": (1 - half) * 2 + core}
    partner = {"seq": 1 - s}
    diagonal = {"dp": twin, "seq": 1 - s}
    native = core == s
    foreign = core != s
    inner = (f > 0) & (f < nf - 1)
    first = 1 + f % 2
    second = (2 + 3 * f) % 5
    third = 6 - f - first - second
    end = 3 * (f - 1)
    outer = jnp.logical_not(inner)
    corner = {"dp": (1 - half) * 2 + core, "seq": 1 - s}

    def remote(src, dst, send, recv, device):
        return pltpu.make_async_remote_copy(
            src_ref=src,
            dst_ref=dst,
            send_sem=send,
            recv_sem=recv,
            device_id=device,
            device_id_type=pl.DeviceIdType.MESH,
        )

    def wait_into(ref, sem):
        pltpu.make_async_copy(ref, ref, sem).wait()

    def head_cols(g, c):
        return pl.ds(pl.multiple_of(g * rows + c * core_rows, core_rows), core_rows)

    def chunk_cols(k):
        return slice(starts[k], starts[k] + widths[k])

    def chunk(k):
        return c_hbm.at[:, starts[k] : starts[k] + widths[k]]

    def group_at(i):
        return (f + 1 + i) % nf

    def near_local(which, g):
        src = (q_hbm, k_hbm, v_hbm)[which]
        return pltpu.make_async_copy(
            src.at[:, head_cols(g, core)], qkv.at[which, g, s], in_recv.at[which, g, s]
        )

    def near_copy(which, g):
        src = (q_hbm, k_hbm, v_hbm)[which]
        return remote(
            src.at[:, head_cols(g, core)],
            qkv.at[which, g, s],
            in_send.at[0, which, g],
            in_recv.at[which, g, s],
            {"seq": core},
        )

    def far_copy(which, g):
        src = (q_hbm, k_hbm, v_hbm)[which]
        return remote(
            src.at[:, head_cols(g, 1 - core)],
            qkv.at[which, g, s],
            in_send.at[1, which, g],
            in_recv.at[which, g, s],
            {"dp": twin, "seq": core},
        )

    def own_local(k):
        return pltpu.make_async_copy(chunk(k), cot[k].at[f, core], cot_recv.at[f, core, k])

    def own_z(lane, k, src):
        return remote(
            src,
            cot[k].at[f, core],
            cot_z.at[lane, k],
            cot_recv.at[f, core, k],
            {"fsdp": (first, second)[lane]},
        )

    def to_sibling(j, k, src):
        return remote(src, cot[k].at[j, core], cot_sib.at[j, k], cot_recv.at[j, core, k], sibling)

    def cross(k):
        return remote(
            chunk(k), cot[k].at[f, 1 - core], cot_x.at[k], cot_recv.at[f, 1 - core, k], diagonal
        )

    def passed(i):
        return (3 - f) + i * (3 - 2 * f)

    def pass_on(i, k):
        j = passed(i)
        block = cot[k].at[j, core]
        return remote(block, block, cot_fw.at[i, k], cot_recv.at[j, core, k], {"fsdp": end})

    def go_copy(j):
        return remote(go_out.at[j], go_in.at[f], go_send.at[j], go_recv.at[f], {"fsdp": j})

    def at_copy(j):
        return remote(at_out.at[j], at_in.at[f], at_send.at[j], at_recv.at[f], {"fsdp": j})

    def home_local(g):
        return pltpu.make_async_copy(
            grads.at[g, s], gr_ref.at[:, :, head_cols(g, core)], out_recv.at[g, core]
        )

    def home_copy(g, t):
        return remote(
            grads.at[g, t],
            gr_ref.at[:, :, head_cols(g, core)],
            out_send.at[g, t],
            out_recv.at[g, core],
            {"dp": half * 2 + s, "seq": t},
        )

    w_load = pltpu.make_async_copy(
        w_hbm.at[pl.ds(pl.multiple_of(core * core_rows, core_rows), core_rows), :], w_ref, w_sem
    )

    @pl.when(native)
    def _():
        for i in range(nf):
            for which in range(3):
                near_local(which, group_at(i)).start()

    barrier = pltpu.get_barrier_semaphore()
    for device in (sibling, across, partner, diagonal, corner):
        pl.semaphore_signal(
            barrier, inc=1, device_id=device, device_id_type=pl.DeviceIdType.MESH
        )
    for step in range(1, nf):
        pl.semaphore_signal(
            barrier,
            inc=1,
            device_id={"fsdp": (f + step) % nf},
            device_id_type=pl.DeviceIdType.MESH,
        )
    pl.semaphore_wait(barrier, 5 + nf - 1)

    @pl.when(native)
    def _():
        for k in range(CHUNKS):
            own_z(0, k, chunk(k)).start()
            own_z(1, k, chunk(k)).start()
        for i in range(nf):
            for which in range(3):
                far_copy(which, group_at(i)).start()
        for k in range(CHUNKS):
            own_local(k).start()
            to_sibling(f, k, chunk(k)).start()

    @pl.when(foreign)
    def _():
        for i in range(nf):
            for which in range(3):
                near_copy(which, group_at(i)).start()
                far_copy(which, group_at(i)).start()
            cross(i).start()

    w_load.start()

    def head_of(which, g, inner_cols):
        return qkv[which, g, :, :, inner_cols].reshape(length, DH)

    def soften(i):
        g = group_at(i)
        for which in range(3):
            for t in range(2):
                wait_into(qkv.at[which, g, t], in_recv.at[which, g, t])
        for t in range(group_heads):
            cols = slice(t * DH, (t + 1) * DH)
            scores = dot_nt(head_of(0, g, cols), head_of(1, g, cols))
            highest = jnp.max(scores, axis=1, keepdims=True)
            expanded = jnp.exp2((scores - highest) * (scale * LOG2E))
            weights = expanded * (1.0 / jnp.sum(expanded, axis=1, keepdims=True))
            probs[g * group_heads + t] = weights
            at_out[g, :, cols] = dot_nn(weights.astype(BF16), head_of(2, g, cols)).astype(BF16)
        if i == nf - 1:
            at_in[f] = at_out[f]
        else:
            at_copy(g).start()

    def differentiate(g):
        for t in range(group_heads):
            cols = slice(t * DH, (t + 1) * DH)
            qh, kh, vh = (head_of(which, g, cols) for which in range(3))
            gh = go_in[g, :, cols]
            weights = probs[g * group_heads + t]
            grad_weights = dot_nt(gh, vh)
            delta = jnp.sum(weights * grad_weights, axis=1, keepdims=True)
            grad_scores = (weights * (grad_weights - delta)).astype(BF16)
            results = (
                dot_nn(grad_scores, kh) * scale,
                dot_tn(grad_scores, qh) * scale,
                dot_tn(weights.astype(BF16), gh),
            )
            for which, result in enumerate(results):
                grads[g, :, which, :, cols] = result.astype(BF16).reshape(2, tokens, DH)
        home_copy(g, 1 - s).start()

        @pl.when(native)
        def _():
            home_local(g).start()

        @pl.when(foreign)
        def _():
            home_copy(g, s).start()

    def project(j):
        total = None
        for k in range(CHUNKS):
            term = dot_nt(
                cot[k][j].reshape(length, widths[k]), w_ref[:, starts[k] : starts[k] + widths[k]]
            )
            total = term if total is None else total + term
        return total.astype(BF16)

    def take(j, k):
        wait_into(cot[k].at[j, core], cot_recv.at[j, core, k])

    def take_other(j, k):
        wait_into(cot[k].at[j, 1 - core], cot_recv.at[j, 1 - core, k])

    def share(j, k):
        take(j, k)
        to_sibling(j, k, cot[k].at[j, core]).start()

    def urgent(k):
        @pl.when(inner)
        def _():
            for i in range(2):
                j = passed(i)
                take(j, k)
                pass_on(i, k).start()
                to_sibling(j, k, cot[k].at[j, core]).start()

    def pass_own(k):
        take(f, k)
        own_z(0, k, cot[k].at[f, core]).start()
        own_z(1, k, cot[k].at[f, core]).start()
        to_sibling(f, k, cot[k].at[f, core]).start()

    def for_native(*chunks):
        @pl.when(native)
        def _():
            for k in chunks:
                urgent(k)

    def for_foreign(*chunks):
        @pl.when(foreign)
        def _():
            for k in chunks:
                urgent(k)

    def for_own(k):
        @pl.when(foreign)
        def _():
            pass_own(k)

    for_native(0)
    soften(0)
    for_native(1)
    for_own(0)
    soften(1)
    for_native(2)
    for_own(1)
    soften(2)
    for_native(3)
    for_own(2)
    for_foreign(0)
    soften(3)
    for_own(3)

    @pl.when(native)
    def _():
        for k in range(CHUNKS):
            take(f, k)

    for k in range(CHUNKS):
        take_other(f, k)
    w_load.wait()
    go_in[f] = project(f)
    differentiate(f)

    def mine():
        return pl.ds(pl.multiple_of(half * half_rows, half_rows), half_rows)

    def theirs():
        return pl.ds(pl.multiple_of((1 - half) * half_rows, half_rows), half_rows)

    def reduce_copy(stage, c):
        src, dst = ((y_out, y_in), (x_out, x_in))[stage]
        device = (across, partner)[stage]
        return remote(src[c], dst[c], rs_send.at[stage, c], rs_recv.at[stage, c], device)

    def gather_copy(stage, c):
        which = half if stage < 2 else 1 - half
        base = core * core_rows + which * half_rows
        block = final.at[pl.ds(pl.multiple_of(base, half_rows), half_rows), chunk_cols(c)]
        device = (across, sibling, sibling)[stage]
        return remote(block, block, ag_send.at[stage, c], ag_recv.at[stage, c], device)

    last = CHUNKS - 1

    def quarter_of(h, t):
        count = half_rows // 2
        return pl.ds(pl.multiple_of((h * 2 + t) * count, count), count)

    others = ((half, 1 - s, partner), (1 - half, s, across), (1 - half, 1 - s, corner))

    def direct_copy(i):
        h, t, device = others[i]
        return remote(d_out.at[quarter_of(h, t)], d_in.at[i], ds_send.at[i], ds_recv.at[i], device)

    def piece(c, h, t):
        base = core * core_rows + (h * 2 + t) * (half_rows // 2)
        return final.at[pl.ds(pl.multiple_of(base, half_rows // 2), half_rows // 2), chunk_cols(last)]

    def spread_copy(i):
        block = piece(core, half, s)
        device = (partner, across, corner, sibling)[i]
        return remote(block, block, dg_send.at[i], dg_recv.at[i], device)

    def relay_copy(i):
        h, t, _ = others[i]
        block = piece(core, h, t)
        return remote(block, block, df_send.at[i], df_recv.at[i], sibling)

    def weight_term(c):
        if c == 0:
            for d in (first, second, third):
                wait_into(at_in.at[d], at_recv.at[d])
        at_all = at_in[...].reshape(nf * length, core_rows)
        acc[c][...] = dot_tn(at_all, cot[c][...].reshape(nf * length, widths[c]))
        if c < last:
            y_out[c][...] = acc[c][theirs()].astype(BF16)
            reduce_copy(0, c).start()
        else:
            d_out[...] = acc[c][...].astype(BF16)
            for i in (2, 1, 0):
                direct_copy(i).start()

    def reduce_direct(c):
        total = acc[last][quarter_of(half, s)]
        for i in range(3):
            direct_copy(i).wait_recv()
            total = total + d_in[i].astype(F32)
        piece(core, half, s)[...] = total.astype(BF16)
        for i in (2, 1, 0, 3):
            spread_copy(i).start()

    def gather_direct(c):
        for i in range(3):
            spread_copy(i).wait_recv()
            relay_copy(i).start()

    def gather_last(c):
        spread_copy(3).wait_recv()
        for i in range(3):
            relay_copy(i).wait_recv()

    def reduce_y(c):
        reduce_copy(0, c).wait_recv()
        x_out[c][...] = (acc[c][mine()] + y_in[c][...].astype(F32)).astype(BF16)
        reduce_copy(1, c).start()

    def reduce_x(c):
        reduce_copy(1, c).wait_recv()
        base = core * core_rows + half * half_rows
        final[pl.ds(pl.multiple_of(base, half_rows), half_rows), chunk_cols(c)] = (
            x_out[c][...].astype(F32) + x_in[c][...].astype(F32)
        ).astype(BF16)
        gather_copy(0, c).start()
        gather_copy(1, c).start()

    def gather_y(c):
        gather_copy(0, c).wait_recv()
        gather_copy(2, c).start()

    def gather_core(c):
        gather_copy(1, c).wait_recv()
        gather_copy(2, c).wait_recv()

    def send_go(j):
        go_out[j] = project(j)
        go_copy(j).start()

    def take_go(j):
        wait_into(go_in.at[j], go_recv.at[j])
        differentiate(j)

    def arrive(j, k):
        share(j, k)
        take_other(j, k)

    def all_arrive(k):
        for j in (first, second, third):
            share(j, k)
        for j in (first, second, third):
            take_other(j, k)

    def end_arrives(k):
        arrive(second, k)

    def passed_arrive(k):
        if k > 0:
            for_foreign(k)
        take_other(first, k)
        take_other(third, k)

    def settle(c):
        for g in range(nf):
            for which in range(3):
                far_copy(which, g).wait_send()
        for j in (first, second, third):
            at_copy(j).wait_send()
        for k in range(CHUNKS):
            own_z(0, k, cot[k].at[f, core]).wait_send()
            own_z(1, k, cot[k].at[f, core]).wait_send()
            to_sibling(f, k, cot[k].at[f, core]).wait_send()

        @pl.when(foreign)
        def _():
            for g in range(nf):
                for which in range(3):
                    near_copy(which, g).wait_send()
            for k in range(CHUNKS):
                cross(k).wait_send()

    def play(*steps):
        for action, argument in steps:
            action(argument)

    @pl.when(inner)
    def _():
        play(
            (end_arrives, 0),
            (passed_arrive, 0),
            (weight_term, 0),
            (end_arrives, 1),
            (passed_arrive, 1),
            (weight_term, 1),
            (end_arrives, 2),
            (end_arrives, 3),
            (send_go, second),
            (reduce_y, 0),
            (passed_arrive, 2),
            (weight_term, 2),
            (reduce_y, 1),
            (passed_arrive, 3),
            (weight_term, 3),
            (send_go, third),
            (send_go, first),
            (reduce_y, 2),
            (reduce_x, 0),
            (reduce_x, 1),
            (reduce_direct, last),
            (reduce_x, 2),
            (settle, 0),
            (take_go, first),
            (gather_direct, last),
            (gather_y, 0),
            (gather_core, 0),
            (gather_y, 1),
            (gather_core, 1),
            (gather_last, last),
            (gather_y, 2),
            (gather_core, 2),
            (take_go, second),
            (take_go, third),
        )

    @pl.when(outer)
    def _():
        play(
            (all_arrive, 0),
            (weight_term, 0),
            (all_arrive, 1),
            (weight_term, 1),
            (reduce_y, 0),
            (take_go, first),
            (all_arrive, 2),
            (weight_term, 2),
            (reduce_y, 1),
            (reduce_x, 0),
            (settle, 0),
            (all_arrive, 3),
            (weight_term, 3),
            (send_go, first),
            (send_go, second),
            (send_go, third),
            (reduce_y, 2),
            (reduce_x, 1),
            (take_go, second),
            (reduce_direct, last),
            (reduce_x, 2),
            (take_go, third),
            (gather_direct, last),
            (gather_y, 0),
            (gather_core, 0),
            (gather_y, 1),
            (gather_core, 1),
            (gather_last, last),
            (gather_y, 2),
            (gather_core, 2),
        )

    for g in range(nf):
        for c in range(2):
            wait_into(gr_ref.at[:, :, head_cols(g, c)], out_recv.at[g, c])
    for c in range(CHUNKS):
        if c == last:
            continue
        for stage in range(2):
            reduce_copy(stage, c).wait_send()
        for stage in range(3):
            gather_copy(stage, c).wait_send()
    for i in range(3):
        direct_copy(i).wait_send()
        relay_copy(i).wait_send()
    for i in range(4):
        spread_copy(i).wait_send()
    for j in (first, second, third):
        go_copy(j).wait_send()
    for g in range(nf):
        home_copy(g, 1 - s).wait_send()
    for k in range(CHUNKS):
        for j in (first, second, third):
            to_sibling(j, k, cot[k].at[j, core]).wait_send()

    @pl.when(inner)
    def _():
        for k in range(CHUNKS):
            for i in range(2):
                pass_on(i, k).wait_send()

    @pl.when(foreign)
    def _():
        for g in range(nf):
            home_copy(g, s).wait_send()


def store_kernel(factor, gr, wg, qg_out, kg_out, vg_out, wg_out, wide, sems, out_sems):
    count = wg.shape[0] // STORES
    copies = [
        pltpu.make_async_copy(gr.at[i], dst, sems.at[i])
        for i, dst in enumerate((qg_out, kg_out, vg_out))
    ]
    for i in range(STORES):
        block = slice(i * count, (i + 1) * count)
        wide[i] = wg[block].astype(F32) * factor
        pltpu.make_async_copy(wide.at[i], wg_out.at[block], out_sems.at[i]).start()
        if i < 3:
            copies[i].start()
    for i in range(STORES):
        block = slice(i * count, (i + 1) * count)
        pltpu.make_async_copy(wide.at[i], wg_out.at[block], out_sems.at[i]).wait()
    for copy in copies:
        copy.wait()


def fused_body(nf, queries, key_rows, value_rows, cotangent, out_weight):
    samples = lax.axis_size("dp") * nf
    tokens, heads_width = queries.shape[1:]
    rows, width = out_weight.shape
    widths = chunk_widths(width)[0]
    core_rows = rows // 2
    half_rows = core_rows // 2
    length = 2 * tokens
    heads = heads_width // DH // 2
    dma = pltpu.SemaphoreType.DMA
    outs = pl.pallas_call(
        functools.partial(fused_kernel, nf),
        out_shape=(
            pltpu.VMEM((3, tokens, heads_width), BF16),
            pltpu.VMEM((rows, width), BF16),
        ),
        in_specs=[pl.BlockSpec(memory_space=pltpu.HBM)] * 5,
        out_specs=[pl.BlockSpec(memory_space=pltpu.VMEM)] * 2,
        scratch_shapes=[
            tuple(pltpu.VMEM((nf, 2, tokens, part), BF16) for part in widths),
            pltpu.VMEM((3, nf, 2, tokens, core_rows), BF16),
            pltpu.VMEM((nf, length, core_rows), BF16),
            pltpu.VMEM((nf, length, core_rows), BF16),
            pltpu.VMEM((nf, length, core_rows), BF16),
            pltpu.VMEM((nf, length, core_rows), BF16),
            pltpu.VMEM((heads, length, length), F32),
            pltpu.VMEM((nf, 2, 3, tokens, core_rows), BF16),
            pltpu.VMEM((core_rows, width), BF16),
            tuple(pltpu.VMEM((core_rows, part), F32) for part in widths),
            tuple(pltpu.VMEM((half_rows, part), BF16) for part in widths),
            tuple(pltpu.VMEM((half_rows, part), BF16) for part in widths),
            tuple(pltpu.VMEM((half_rows, part), BF16) for part in widths),
            tuple(pltpu.VMEM((half_rows, part), BF16) for part in widths),
            pltpu.VMEM((core_rows, widths[-1]), BF16),
            pltpu.VMEM((3, half_rows // 2, widths[-1]), BF16),
            dma,
            dma((2, 3, nf)),
            dma((3, nf, 2)),
            dma((2, CHUNKS)),
            dma((2, CHUNKS)),
            dma((nf, CHUNKS)),
            dma((CHUNKS,)),
            dma((nf, 2, CHUNKS)),
            dma((nf,)),
            dma((nf,)),
            dma((nf,)),
            dma((nf,)),
            dma((nf, 2)),
            dma((nf, 2)),
            dma((2, CHUNKS)),
            dma((2, CHUNKS)),
            dma((3, CHUNKS)),
            dma((3, CHUNKS)),
            dma((3,)),
            dma((3,)),
            dma((4,)),
            dma((4,)),
            dma((3,)),
            dma((3,)),
        ],
        compiler_params=pltpu.CompilerParams(
            collective_id=0, has_side_effects=True, vmem_limit_bytes=58 * 1024 * 1024
        ),
    )(queries[0], key_rows[0], value_rows[0], cotangent[0], out_weight)
    stored = pl.pallas_call(
        functools.partial(store_kernel, 1.0 / samples),
        out_shape=(jax.ShapeDtypeStruct((tokens, heads_width), BF16),) * 3
        + (jax.ShapeDtypeStruct((rows, width), F32),),
        in_specs=[pl.BlockSpec(memory_space=pltpu.VMEM)] * 2,
        out_specs=[pl.BlockSpec(memory_space=pltpu.HBM)] * 4,
        scratch_shapes=[
            pltpu.VMEM((STORES, rows // STORES, width), F32),
            dma((3,)),
            dma((STORES,)),
        ],
        compiler_params=pltpu.CompilerParams(vmem_limit_bytes=24 * 1024 * 1024),
    )(*outs)
    return tuple(out[None] for out in stored[:3]) + (stored[3],)


def pick_body(mesh):
    if mesh.shape["seq"] == 2 and mesh.shape["dp"] == 4 and mesh.shape["fsdp"] == 4:
        return functools.partial(fused_body, mesh.shape["fsdp"])
    return body


def solution(mesh):
    return jax.shard_map(
        pick_body(mesh),
        mesh=mesh,
        in_specs=(
            P(("dp", "fsdp"), "seq", None),
            P(("dp", "fsdp"), "seq", None),
            P(("dp", "fsdp"), "seq", None),
            P(("dp", "fsdp"), "seq", None),
            P("fsdp", None),
        ),
        out_specs=(
            P(("dp", "fsdp"), "seq", None),
            P(("dp", "fsdp"), "seq", None),
            P(("dp", "fsdp"), "seq", None),
            P("fsdp", None),
        ),
        check_vma=False,
    )
```

```python
import functools

import jax
import jax.numpy as jnp
from jax import lax
from jax.experimental import pallas as pl
from jax.experimental.pallas import tpu as pltpu
from jax.sharding import PartitionSpec as P

DH = 128
LOG2E = 1.4426950408889634
SHARES = (5, 4, 4, 3)
CHUNKS = len(SHARES)
STORES = 8
F32 = jnp.float32
BF16 = jnp.bfloat16


def head_backward(query_head, key_head, value_head, grad_head, block_rows):
    length = key_head.shape[0]
    score_scale = DH ** (-0.5)
    blocks = length // block_rows

    def visit(carry, block):
        key_acc, value_acc = carry
        begin = block * block_rows
        query_block = lax.dynamic_slice_in_dim(query_head, begin, block_rows, 0)
        grad_block = lax.dynamic_slice_in_dim(grad_head, begin, block_rows, 0)
        scores = (
            jnp.einsum("qd,kd->qk", query_block, key_head, preferred_element_type=jnp.float32)
            * score_scale
        )
        highest = jnp.max(scores, axis=1, keepdims=True)
        expanded = jnp.exp(scores - highest)
        weights = expanded / jnp.sum(expanded, axis=1, keepdims=True)
        weights_half = weights.astype(jnp.bfloat16)
        attended = jnp.einsum(
            "qk,kd->qd", weights_half, value_head, preferred_element_type=jnp.float32
        ).astype(jnp.bfloat16)
        grad_weights = jnp.einsum(
            "qd,kd->qk", grad_block, value_head, preferred_element_type=jnp.float32
        )
        row_delta = jnp.sum(weights * grad_weights, axis=1, keepdims=True)
        grad_scores = (weights * (grad_weights - row_delta)).astype(jnp.bfloat16)
        query_grad = (
            jnp.einsum("qk,kd->qd", grad_scores, key_head, preferred_element_type=jnp.float32)
            * score_scale
        ).astype(jnp.bfloat16)
        key_acc = key_acc + jnp.einsum(
            "qk,qd->kd", grad_scores, query_block, preferred_element_type=jnp.float32
        )
        value_acc = value_acc + jnp.einsum(
            "qk,qd->kd", weights_half, grad_block, preferred_element_type=jnp.float32
        )
        return ((key_acc, value_acc), (attended, query_grad))

    empty = jnp.zeros(key_head.shape, jnp.float32)
    finals, stacked = lax.scan(visit, (empty, empty), jnp.arange(blocks))
    attended = stacked[0].reshape(length, DH)
    query_grad = stacked[1].reshape(length, DH)
    key_grad = (finals[0] * score_scale).astype(jnp.bfloat16)
    value_grad = finals[1].astype(jnp.bfloat16)
    return (attended, query_grad, key_grad, value_grad)


def attend_heads(query_heads, key_heads, value_heads, grad_heads):
    length = query_heads.shape[1]
    per_device = query_heads.shape[2] // DH
    block_rows = min(512, length)
    gathered = [[], [], [], []]
    for head_index in range(per_device):
        lower = head_index * DH
        upper = lower + DH
        results = head_backward(
            query_heads[0, :, lower:upper],
            key_heads[0, :, lower:upper],
            value_heads[0, :, lower:upper],
            grad_heads[0, :, lower:upper],
            block_rows,
        )
        for position, result in enumerate(results):
            gathered[position].append(result)
    return tuple((jnp.concatenate(group, axis=1)[None] for group in gathered))


def body(queries, key_rows, value_rows, cotangent, out_weight):
    samples = lax.axis_size("dp") * lax.axis_size("fsdp")
    grad_out = jnp.einsum(
        "btd,rd->btr",
        cotangent,
        lax.all_gather(out_weight, "fsdp", axis=0, tiled=True),
        preferred_element_type=jnp.float32,
    ).astype(jnp.bfloat16)
    query_heads, key_heads, value_heads, grad_heads = (
        lax.all_to_all(queries, "seq", split_axis=2, concat_axis=1, tiled=True),
        lax.all_to_all(key_rows, "seq", split_axis=2, concat_axis=1, tiled=True),
        lax.all_to_all(value_rows, "seq", split_axis=2, concat_axis=1, tiled=True),
        lax.all_to_all(grad_out, "seq", split_axis=2, concat_axis=1, tiled=True),
    )
    head_results = attend_heads(query_heads, key_heads, value_heads, grad_heads)
    attended, query_grad, key_grad, value_grad = (
        lax.all_to_all(head_results[0], "seq", split_axis=1, concat_axis=2, tiled=True),
        lax.all_to_all(head_results[1], "seq", split_axis=1, concat_axis=2, tiled=True),
        lax.all_to_all(head_results[2], "seq", split_axis=1, concat_axis=2, tiled=True),
        lax.all_to_all(head_results[3], "seq", split_axis=1, concat_axis=2, tiled=True),
    )
    shares = lax.psum_scatter(
        jnp.einsum("btr,btd->rd", attended, cotangent, preferred_element_type=jnp.float32),
        ("fsdp", "seq"),
        scatter_dimension=0,
        tiled=True,
    )
    shares = lax.psum(shares.astype(jnp.bfloat16), "dp").astype(jnp.float32)
    total = lax.all_gather(shares.astype(jnp.bfloat16), "seq", axis=0, tiled=True).astype(
        shares.dtype
    )
    return (query_grad, key_grad, value_grad, total / samples)


def dot_nn(a, b):
    return lax.dot_general(a, b, (((1,), (0,)), ((), ())), preferred_element_type=F32)


def dot_nt(a, b):
    return lax.dot_general(a, b, (((1,), (1,)), ((), ())), preferred_element_type=F32)


def dot_tn(a, b):
    return lax.dot_general(a, b, (((0,), (0,)), ((), ())), preferred_element_type=F32)


def chunk_widths(width):
    unit = width // sum(SHARES)
    widths = [share * unit for share in SHARES]
    return widths, [sum(widths[:k]) for k in range(CHUNKS)]


def fused_kernel(
    nf,
    q_hbm,
    k_hbm,
    v_hbm,
    c_hbm,
    w_hbm,
    gr_ref,
    final,
    cot,
    qkv,
    go_out,
    go_in,
    at_out,
    at_in,
    probs,
    grads,
    w_ref,
    acc,
    y_out,
    y_in,
    x_out,
    x_in,
    d_out,
    d_in,
    w_sem,
    in_send,
    in_recv,
    cot_z,
    cot_fw,
    cot_sib,
    cot_x,
    cot_recv,
    go_send,
    go_recv,
    at_send,
    at_recv,
    out_send,
    out_recv,
    rs_send,
    rs_recv,
    ag_send,
    ag_recv,
    ds_send,
    ds_recv,
    dg_send,
    dg_recv,
    df_send,
    df_recv,
):
    tokens, width = c_hbm.shape
    rows = w_hbm.shape[0]
    widths, starts = chunk_widths(width)
    core_rows = rows // 2
    half_rows = core_rows // 2
    group_heads = core_rows // DH
    length = 2 * tokens
    scale = DH ** (-0.5)
    dp = lax.axis_index("dp")
    f = lax.axis_index("fsdp")
    s = lax.axis_index("seq")
    core = dp % 2
    half = dp // 2
    twin = half * 2 + (1 - core)
    sibling = {"dp": twin}
    across = {"dp": (1 - half) * 2 + core}
    partner = {"seq": 1 - s}
    diagonal = {"dp": twin, "seq": 1 - s}
    native = core == s
    foreign = core != s
    inner = (f > 0) & (f < nf - 1)
    first = 1 + f % 2
    second = (2 + 3 * f) % 5
    third = 6 - f - first - second
    end = 3 * (f - 1)
    outer = jnp.logical_not(inner)
    corner = {"dp": (1 - half) * 2 + core, "seq": 1 - s}

    def remote(src, dst, send, recv, device):
        return pltpu.make_async_remote_copy(
            src_ref=src,
            dst_ref=dst,
            send_sem=send,
            recv_sem=recv,
            device_id=device,
            device_id_type=pl.DeviceIdType.MESH,
        )

    def wait_into(ref, sem):
        pltpu.make_async_copy(ref, ref, sem).wait()

    def head_cols(g, c):
        return pl.ds(pl.multiple_of(g * rows + c * core_rows, core_rows), core_rows)

    def chunk_cols(k):
        return slice(starts[k], starts[k] + widths[k])

    def chunk(k):
        return c_hbm.at[:, starts[k] : starts[k] + widths[k]]

    def group_at(i):
        return (f + 1 + i) % nf

    def near_local(which, g):
        src = (q_hbm, k_hbm, v_hbm)[which]
        return pltpu.make_async_copy(
            src.at[:, head_cols(g, core)], qkv.at[which, g, s], in_recv.at[which, g, s]
        )

    def near_copy(which, g):
        src = (q_hbm, k_hbm, v_hbm)[which]
        return remote(
            src.at[:, head_cols(g, core)],
            qkv.at[which, g, s],
            in_send.at[0, which, g],
            in_recv.at[which, g, s],
            {"seq": core},
        )

    def far_copy(which, g):
        src = (q_hbm, k_hbm, v_hbm)[which]
        return remote(
            src.at[:, head_cols(g, 1 - core)],
            qkv.at[which, g, s],
            in_send.at[1, which, g],
            in_recv.at[which, g, s],
            {"dp": twin, "seq": core},
        )

    def own_local(k):
        return pltpu.make_async_copy(chunk(k), cot[k].at[f, core], cot_recv.at[f, core, k])

    def own_z(lane, k, src):
        return remote(
            src,
            cot[k].at[f, core],
            cot_z.at[lane, k],
            cot_recv.at[f, core, k],
            {"fsdp": (first, second)[lane]},
        )

    def to_sibling(j, k, src):
        return remote(src, cot[k].at[j, core], cot_sib.at[j, k], cot_recv.at[j, core, k], sibling)

    def cross(k):
        return remote(
            chunk(k), cot[k].at[f, 1 - core], cot_x.at[k], cot_recv.at[f, 1 - core, k], diagonal
        )

    def passed(i):
        return (3 - f) + i * (3 - 2 * f)

    def pass_on(i, k):
        j = passed(i)
        block = cot[k].at[j, core]
        return remote(block, block, cot_fw.at[i, k], cot_recv.at[j, core, k], {"fsdp": end})

    def go_copy(j):
        return remote(go_out.at[j], go_in.at[f], go_send.at[j], go_recv.at[f], {"fsdp": j})

    def at_copy(j):
        return remote(at_out.at[j], at_in.at[f], at_send.at[j], at_recv.at[f], {"fsdp": j})

    def home_local(g):
        return pltpu.make_async_copy(
            grads.at[g, s], gr_ref.at[:, :, head_cols(g, core)], out_recv.at[g, core]
        )

    def home_copy(g, t):
        return remote(
            grads.at[g, t],
            gr_ref.at[:, :, head_cols(g, core)],
            out_send.at[g, t],
            out_recv.at[g, core],
            {"dp": half * 2 + s, "seq": t},
        )

    w_load = pltpu.make_async_copy(
        w_hbm.at[pl.ds(pl.multiple_of(core * core_rows, core_rows), core_rows), :], w_ref, w_sem
    )

    @pl.when(native)
    def _():
        for i in range(nf):
            for which in range(3):
                near_local(which, group_at(i)).start()

    barrier = pltpu.get_barrier_semaphore()
    for device in (sibling, across, partner, diagonal, corner):
        pl.semaphore_signal(
            barrier, inc=1, device_id=device, device_id_type=pl.DeviceIdType.MESH
        )
    for step in range(1, nf):
        pl.semaphore_signal(
            barrier,
            inc=1,
            device_id={"fsdp": (f + step) % nf},
            device_id_type=pl.DeviceIdType.MESH,
        )
    pl.semaphore_wait(barrier, 5 + nf - 1)

    @pl.when(native)
    def _():
        for k in range(CHUNKS):
            own_z(0, k, chunk(k)).start()
            own_z(1, k, chunk(k)).start()
        for i in range(nf):
            for which in range(3):
                far_copy(which, group_at(i)).start()
        for k in range(CHUNKS):
            own_local(k).start()
            to_sibling(f, k, chunk(k)).start()

    @pl.when(foreign)
    def _():
        for i in range(nf):
            for which in range(3):
                near_copy(which, group_at(i)).start()
                far_copy(which, group_at(i)).start()
            cross(i).start()

    w_load.start()

    def head_of(which, g, inner_cols):
        return qkv[which, g, :, :, inner_cols].reshape(length, DH)

    def soften(i):
        g = group_at(i)
        for which in range(3):
            for t in range(2):
                wait_into(qkv.at[which, g, t], in_recv.at[which, g, t])
        for t in range(group_heads):
            cols = slice(t * DH, (t + 1) * DH)
            scores = dot_nt(head_of(0, g, cols), head_of(1, g, cols))
            highest = jnp.max(scores, axis=1, keepdims=True)
            expanded = jnp.exp2((scores - highest) * (scale * LOG2E))
            weights = expanded * (1.0 / jnp.sum(expanded, axis=1, keepdims=True))
            probs[g * group_heads + t] = weights
            at_out[g, :, cols] = dot_nn(weights.astype(BF16), head_of(2, g, cols)).astype(BF16)
        if i == nf - 1:
            at_in[f] = at_out[f]
        else:
            at_copy(g).start()

    def differentiate(g):
        for t in range(group_heads):
            cols = slice(t * DH, (t + 1) * DH)
            qh, kh, vh = (head_of(which, g, cols) for which in range(3))
            gh = go_in[g, :, cols]
            weights = probs[g * group_heads + t]
            grad_weights = dot_nt(gh, vh)
            delta = jnp.sum(weights * grad_weights, axis=1, keepdims=True)
            grad_scores = (weights * (grad_weights - delta)).astype(BF16)
            results = (
                dot_nn(grad_scores, kh) * scale,
                dot_tn(grad_scores, qh) * scale,
                dot_tn(weights.astype(BF16), gh),
            )
            for which, result in enumerate(results):
                grads[g, :, which, :, cols] = result.astype(BF16).reshape(2, tokens, DH)
        home_copy(g, 1 - s).start()

        @pl.when(native)
        def _():
            home_local(g).start()

        @pl.when(foreign)
        def _():
            home_copy(g, s).start()

    def project(j):
        total = None
        for k in range(CHUNKS):
            term = dot_nt(
                cot[k][j].reshape(length, widths[k]), w_ref[:, starts[k] : starts[k] + widths[k]]
            )
            total = term if total is None else total + term
        return total.astype(BF16)

    def take(j, k):
        wait_into(cot[k].at[j, core], cot_recv.at[j, core, k])

    def take_other(j, k):
        wait_into(cot[k].at[j, 1 - core], cot_recv.at[j, 1 - core, k])

    def share(j, k):
        take(j, k)
        to_sibling(j, k, cot[k].at[j, core]).start()

    def urgent(k):
        @pl.when(inner)
        def _():
            for i in range(2):
                j = passed(i)
                take(j, k)
                pass_on(i, k).start()
                to_sibling(j, k, cot[k].at[j, core]).start()

    def pass_own(k):
        take(f, k)
        own_z(0, k, cot[k].at[f, core]).start()
        own_z(1, k, cot[k].at[f, core]).start()
        to_sibling(f, k, cot[k].at[f, core]).start()

    def for_native(*chunks):
        @pl.when(native)
        def _():
            for k in chunks:
                urgent(k)

    def for_foreign(*chunks):
        @pl.when(foreign)
        def _():
            for k in chunks:
                urgent(k)

    def for_own(k):
        @pl.when(foreign)
        def _():
            pass_own(k)

    for_native(0)
    soften(0)
    for_native(1)
    for_own(0)
    soften(1)
    for_native(2)
    for_own(1)
    soften(2)
    for_native(3)
    for_own(2)
    for_foreign(0)
    soften(3)
    for_own(3)

    @pl.when(native)
    def _():
        for k in range(CHUNKS):
            take(f, k)

    for k in range(CHUNKS):
        take_other(f, k)
    w_load.wait()
    go_in[f] = project(f)
    differentiate(f)

    def mine():
        return pl.ds(pl.multiple_of(half * half_rows, half_rows), half_rows)

    def theirs():
        return pl.ds(pl.multiple_of((1 - half) * half_rows, half_rows), half_rows)

    def reduce_copy(stage, c):
        src, dst = ((y_out, y_in), (x_out, x_in))[stage]
        device = (across, partner)[stage]
        return remote(src[c], dst[c], rs_send.at[stage, c], rs_recv.at[stage, c], device)

    def gather_copy(stage, c):
        which = half if stage < 2 else 1 - half
        base = core * core_rows + which * half_rows
        block = final.at[pl.ds(pl.multiple_of(base, half_rows), half_rows), chunk_cols(c)]
        device = (across, sibling, sibling)[stage]
        return remote(block, block, ag_send.at[stage, c], ag_recv.at[stage, c], device)

    last = CHUNKS - 1

    def quarter_of(h, t):
        count = half_rows // 2
        return pl.ds(pl.multiple_of((h * 2 + t) * count, count), count)

    others = ((half, 1 - s, partner), (1 - half, s, across), (1 - half, 1 - s, corner))

    def direct_copy(i):
        h, t, device = others[i]
        return remote(d_out.at[quarter_of(h, t)], d_in.at[i], ds_send.at[i], ds_recv.at[i], device)

    def piece(c, h, t):
        base = core * core_rows + (h * 2 + t) * (half_rows // 2)
        return final.at[pl.ds(pl.multiple_of(base, half_rows // 2), half_rows // 2), chunk_cols(last)]

    def spread_copy(i):
        block = piece(core, half, s)
        device = (partner, across, corner, sibling)[i]
        return remote(block, block, dg_send.at[i], dg_recv.at[i], device)

    def relay_copy(i):
        h, t, _ = others[i]
        block = piece(core, h, t)
        return remote(block, block, df_send.at[i], df_recv.at[i], sibling)

    def weight_term(c):
        if c == 0:
            for d in (first, second, third):
                wait_into(at_in.at[d], at_recv.at[d])
        at_all = at_in[...].reshape(nf * length, core_rows)
        acc[c][...] = dot_tn(at_all, cot[c][...].reshape(nf * length, widths[c]))
        if c < last:
            y_out[c][...] = acc[c][theirs()].astype(BF16)
            reduce_copy(0, c).start()
        else:
            d_out[...] = acc[c][...].astype(BF16)
            for i in (2, 1, 0):
                direct_copy(i).start()

    def reduce_direct(c):
        total = acc[last][quarter_of(half, s)]
        for i in range(3):
            direct_copy(i).wait_recv()
            total = total + d_in[i].astype(F32)
        piece(core, half, s)[...] = total.astype(BF16)
        for i in (2, 1, 0, 3):
            spread_copy(i).start()

    def gather_direct(c):
        for i in range(3):
            spread_copy(i).wait_recv()
            relay_copy(i).start()

    def gather_last(c):
        spread_copy(3).wait_recv()
        for i in range(3):
            relay_copy(i).wait_recv()

    def reduce_y(c):
        reduce_copy(0, c).wait_recv()
        x_out[c][...] = (acc[c][mine()] + y_in[c][...].astype(F32)).astype(BF16)
        reduce_copy(1, c).start()

    def reduce_x(c):
        reduce_copy(1, c).wait_recv()
        base = core * core_rows + half * half_rows
        final[pl.ds(pl.multiple_of(base, half_rows), half_rows), chunk_cols(c)] = (
            x_out[c][...].astype(F32) + x_in[c][...].astype(F32)
        ).astype(BF16)
        gather_copy(0, c).start()
        gather_copy(1, c).start()

    def gather_y(c):
        gather_copy(0, c).wait_recv()
        gather_copy(2, c).start()

    def gather_core(c):
        gather_copy(1, c).wait_recv()
        gather_copy(2, c).wait_recv()

    def send_go(j):
        go_out[j] = project(j)
        go_copy(j).start()

    def take_go(j):
        wait_into(go_in.at[j], go_recv.at[j])
        differentiate(j)

    def arrive(j, k):
        share(j, k)
        take_other(j, k)

    def all_arrive(k):
        for j in (first, second, third):
            share(j, k)
        for j in (first, second, third):
            take_other(j, k)

    def end_arrives(k):
        arrive(second, k)

    def passed_arrive(k):
        if k > 0:
            for_foreign(k)
        take_other(first, k)
        take_other(third, k)

    def settle(c):
        for g in range(nf):
            for which in range(3):
                far_copy(which, g).wait_send()
        for j in (first, second, third):
            at_copy(j).wait_send()
        for k in range(CHUNKS):
            own_z(0, k, cot[k].at[f, core]).wait_send()
            own_z(1, k, cot[k].at[f, core]).wait_send()
            to_sibling(f, k, cot[k].at[f, core]).wait_send()

        @pl.when(foreign)
        def _():
            for g in range(nf):
                for which in range(3):
                    near_copy(which, g).wait_send()
            for k in range(CHUNKS):
                cross(k).wait_send()

    def play(*steps):
        for action, argument in steps:
            action(argument)

    @pl.when(inner)
    def _():
        play(
            (end_arrives, 0),
            (passed_arrive, 0),
            (weight_term, 0),
            (end_arrives, 1),
            (passed_arrive, 1),
            (weight_term, 1),
            (end_arrives, 2),
            (end_arrives, 3),
            (send_go, second),
            (reduce_y, 0),
            (passed_arrive, 2),
            (weight_term, 2),
            (reduce_y, 1),
            (passed_arrive, 3),
            (weight_term, 3),
            (send_go, third),
            (send_go, first),
            (reduce_y, 2),
            (reduce_x, 0),
            (reduce_x, 1),
            (reduce_direct, last),
            (settle, 0),
            (take_go, first),
            (reduce_x, 2),
            (gather_direct, last),
            (gather_y, 0),
            (gather_core, 0),
            (gather_y, 1),
            (gather_core, 1),
            (gather_last, last),
            (gather_y, 2),
            (gather_core, 2),
            (take_go, second),
            (take_go, third),
        )

    @pl.when(outer)
    def _():
        play(
            (all_arrive, 0),
            (weight_term, 0),
            (all_arrive, 1),
            (weight_term, 1),
            (reduce_y, 0),
            (take_go, first),
            (all_arrive, 2),
            (weight_term, 2),
            (reduce_y, 1),
            (reduce_x, 0),
            (settle, 0),
            (all_arrive, 3),
            (weight_term, 3),
            (send_go, first),
            (send_go, second),
            (send_go, third),
            (reduce_y, 2),
            (reduce_x, 1),
            (take_go, second),
            (reduce_direct, last),
            (reduce_x, 2),
            (take_go, third),
            (gather_direct, last),
            (gather_y, 0),
            (gather_core, 0),
            (gather_y, 1),
            (gather_core, 1),
            (gather_last, last),
            (gather_y, 2),
            (gather_core, 2),
        )

    for g in range(nf):
        for c in range(2):
            wait_into(gr_ref.at[:, :, head_cols(g, c)], out_recv.at[g, c])
    for c in range(CHUNKS):
        if c == last:
            continue
        for stage in range(2):
            reduce_copy(stage, c).wait_send()
        for stage in range(3):
            gather_copy(stage, c).wait_send()
    for i in range(3):
        direct_copy(i).wait_send()
        relay_copy(i).wait_send()
    for i in range(4):
        spread_copy(i).wait_send()
    for j in (first, second, third):
        go_copy(j).wait_send()
    for g in range(nf):
        home_copy(g, 1 - s).wait_send()
    for k in range(CHUNKS):
        for j in (first, second, third):
            to_sibling(j, k, cot[k].at[j, core]).wait_send()

    @pl.when(inner)
    def _():
        for k in range(CHUNKS):
            for i in range(2):
                pass_on(i, k).wait_send()

    @pl.when(foreign)
    def _():
        for g in range(nf):
            home_copy(g, s).wait_send()


def store_kernel(factor, gr, wg, qg_out, kg_out, vg_out, wg_out, wide, sems, out_sems):
    count = wg.shape[0] // STORES
    copies = [
        pltpu.make_async_copy(gr.at[i], dst, sems.at[i])
        for i, dst in enumerate((qg_out, kg_out, vg_out))
    ]
    for i in range(STORES):
        block = slice(i * count, (i + 1) * count)
        wide[i] = wg[block].astype(F32) * factor
        pltpu.make_async_copy(wide.at[i], wg_out.at[block], out_sems.at[i]).start()
        if i < 3:
            copies[i].start()
    for i in range(STORES):
        block = slice(i * count, (i + 1) * count)
        pltpu.make_async_copy(wide.at[i], wg_out.at[block], out_sems.at[i]).wait()
    for copy in copies:
        copy.wait()


def fused_body(nf, queries, key_rows, value_rows, cotangent, out_weight):
    samples = lax.axis_size("dp") * nf
    tokens, heads_width = queries.shape[1:]
    rows, width = out_weight.shape
    widths = chunk_widths(width)[0]
    core_rows = rows // 2
    half_rows = core_rows // 2
    length = 2 * tokens
    heads = heads_width // DH // 2
    dma = pltpu.SemaphoreType.DMA
    outs = pl.pallas_call(
        functools.partial(fused_kernel, nf),
        out_shape=(
            pltpu.VMEM((3, tokens, heads_width), BF16),
            pltpu.VMEM((rows, width), BF16),
        ),
        in_specs=[pl.BlockSpec(memory_space=pltpu.HBM)] * 5,
        out_specs=[pl.BlockSpec(memory_space=pltpu.VMEM)] * 2,
        scratch_shapes=[
            tuple(pltpu.VMEM((nf, 2, tokens, part), BF16) for part in widths),
            pltpu.VMEM((3, nf, 2, tokens, core_rows), BF16),
            pltpu.VMEM((nf, length, core_rows), BF16),
            pltpu.VMEM((nf, length, core_rows), BF16),
            pltpu.VMEM((nf, length, core_rows), BF16),
            pltpu.VMEM((nf, length, core_rows), BF16),
            pltpu.VMEM((heads, length, length), F32),
            pltpu.VMEM((nf, 2, 3, tokens, core_rows), BF16),
            pltpu.VMEM((core_rows, width), BF16),
            tuple(pltpu.VMEM((core_rows, part), F32) for part in widths),
            tuple(pltpu.VMEM((half_rows, part), BF16) for part in widths),
            tuple(pltpu.VMEM((half_rows, part), BF16) for part in widths),
            tuple(pltpu.VMEM((half_rows, part), BF16) for part in widths),
            tuple(pltpu.VMEM((half_rows, part), BF16) for part in widths),
            pltpu.VMEM((core_rows, widths[-1]), BF16),
            pltpu.VMEM((3, half_rows // 2, widths[-1]), BF16),
            dma,
            dma((2, 3, nf)),
            dma((3, nf, 2)),
            dma((2, CHUNKS)),
            dma((2, CHUNKS)),
            dma((nf, CHUNKS)),
            dma((CHUNKS,)),
            dma((nf, 2, CHUNKS)),
            dma((nf,)),
            dma((nf,)),
            dma((nf,)),
            dma((nf,)),
            dma((nf, 2)),
            dma((nf, 2)),
            dma((2, CHUNKS)),
            dma((2, CHUNKS)),
            dma((3, CHUNKS)),
            dma((3, CHUNKS)),
            dma((3,)),
            dma((3,)),
            dma((4,)),
            dma((4,)),
            dma((3,)),
            dma((3,)),
        ],
        compiler_params=pltpu.CompilerParams(
            collective_id=0, has_side_effects=True, vmem_limit_bytes=58 * 1024 * 1024
        ),
    )(queries[0], key_rows[0], value_rows[0], cotangent[0], out_weight)
    stored = pl.pallas_call(
        functools.partial(store_kernel, 1.0 / samples),
        out_shape=(jax.ShapeDtypeStruct((tokens, heads_width), BF16),) * 3
        + (jax.ShapeDtypeStruct((rows, width), F32),),
        in_specs=[pl.BlockSpec(memory_space=pltpu.VMEM)] * 2,
        out_specs=[pl.BlockSpec(memory_space=pltpu.HBM)] * 4,
        scratch_shapes=[
            pltpu.VMEM((STORES, rows // STORES, width), F32),
            dma((3,)),
            dma((STORES,)),
        ],
        compiler_params=pltpu.CompilerParams(vmem_limit_bytes=24 * 1024 * 1024),
    )(*outs)
    return tuple(out[None] for out in stored[:3]) + (stored[3],)


def pick_body(mesh):
    if mesh.shape["seq"] == 2 and mesh.shape["dp"] == 4 and mesh.shape["fsdp"] == 4:
        return functools.partial(fused_body, mesh.shape["fsdp"])
    return body


def solution(mesh):
    return jax.shard_map(
        pick_body(mesh),
        mesh=mesh,
        in_specs=(
            P(("dp", "fsdp"), "seq", None),
            P(("dp", "fsdp"), "seq", None),
            P(("dp", "fsdp"), "seq", None),
            P(("dp", "fsdp"), "seq", None),
            P("fsdp", None),
        ),
        out_specs=(
            P(("dp", "fsdp"), "seq", None),
            P(("dp", "fsdp"), "seq", None),
            P(("dp", "fsdp"), "seq", None),
            P("fsdp", None),
        ),
        check_vma=False,
    )
```
